512 devices in a mesh: fsdp: 64 (over y, z), tp: 8 (over x, core).
Axes of the slice: x: 4, y: 8, z: 8, core: 2. Of those that a mesh axis runs over, the one named last changes fastest.
Arguments:
- gradient: bfloat16 [8192, 14336], P('fsdp', 'tp'), may hold values from -50 to 50
- momentum: float32 [8192, 14336], P('fsdp', 'tp'), may hold values from -5 to 5
- right_factor: bfloat16 [14336, 512], P(('tp', 'fsdp')), may hold values from -6 to 6
Outputs:
- update: bfloat16 [8192, 14336], P('fsdp', 'tp')
- momentum_new: float32 [8192, 14336], P('fsdp', 'tp')
- factor_new: bfloat16 [14336, 512], P(('tp', 'fsdp'))
The draws below stay inside these ranges and needn't reach their ends.
All inputs are finite; a program needn't handle non-finite values.
Results may differ from the reference program's by a relative error of at most 0.015.
Values may be sent and summed in bfloat16 or wider, within the bound.
A program may use at most 64 MiB of HBM per device.

```python
import math
import jax
import jax.numpy as jnp
from jax import lax

D = 8192
FFW = 14336
RANK = 512


def draw_gradient(key, part):
    key = jax.random.fold_in(key, 7)
    first, second, third = jax.random.split(key, 3)
    row_trend = jnp.exp(jnp.arange(D, dtype=jnp.float32)[:, None] / D * math.log(3.0))
    col_trend = jnp.exp(jnp.arange(FFW, dtype=jnp.float32)[None, :] / FFW * math.log(3.0))
    row_scale = jnp.exp(jax.random.uniform(first, (D, 1)) * math.log(10.0)) * row_trend
    col_scale = jnp.exp(jax.random.uniform(second, (1, FFW)) * math.log(10.0)) * col_trend
    base = jnp.clip(jax.random.normal(third, (D, FFW)), -2.5, 2.5)
    return (0.01 * base * row_scale * col_scale).astype(jnp.bfloat16)


def draw_momentum(key, part):
    key = jax.random.fold_in(key, 11)
    key_rowgroup, key_colgroup, key_rowscale, key_colscale, key_noise = jax.random.split(key, 5)
    groups = max(2, RANK // 4)
    levels = max(1, groups.bit_length() - 1)
    index_a = jnp.arange(groups, dtype=jnp.int32)[:, None]
    index_b = jnp.arange(groups, dtype=jnp.int32)[None, :]
    parity = jnp.zeros((groups, groups), jnp.int32)
    for bit_level in range(levels):
        parity = parity + index_a // 2 ** bit_level % 2 * (index_b // 2 ** bit_level % 2)
    sign_table = (1 - 2 * (parity % 2)).astype(jnp.float32)
    row_group = jax.random.randint(key_rowgroup, (D,), 0, groups)
    col_group = jax.random.randint(key_colgroup, (FFW,), 0, groups)
    pattern = sign_table[row_group][:, col_group]
    row_scale = jnp.exp(jax.random.uniform(key_rowscale, (D, 1)) * math.log(3.0))
    col_scale = jnp.exp(jax.random.uniform(key_colscale, (1, FFW)) * math.log(3.0))
    noise_part = 0.3 * jnp.clip(jax.random.normal(key_noise, (D, FFW)), -4.0, 4.0)
    return (0.4 * pattern * row_scale * col_scale + noise_part).astype(jnp.float32)


def shard_levels(rng, shape, cuts, least, largest):
    level = 1.0
    for axis_at, parts in cuts:
        draws = jax.random.uniform(jax.random.fold_in(jax.random.fold_in(rng, 6), axis_at), (parts,), jnp.float32, least / len(cuts), largest / len(cuts))
        level = level * jnp.repeat(jnp.exp(draws), shape[axis_at] // parts).reshape((-1,) + (1,) * (len(shape) - 1 - axis_at))
    return level


def normal_values(stream_key, extent, deviation, limit, pieces=(), held_as=jnp.bfloat16):
    entries = deviation * jax.random.normal(stream_key, extent, jnp.float32)
    if pieces:
        entries = entries * shard_levels(stream_key, extent, pieces, -0.22, 0.18)
    return jnp.clip(entries, -limit, limit).astype(held_as)


def setup_inputs(seed: int = 0) -> dict:
    seeds = jax.random.split(jax.random.key(seed), 4)
    gradient = draw_gradient(jax.random.fold_in(seeds[3], 71), 0)
    momentum = draw_momentum(jax.random.fold_in(seeds[3], 71), 0)
    right_factor = normal_values(seeds[2], (FFW, RANK), 1.0, 6.0, ((0, 512),))
    return {"gradient": gradient, "momentum": momentum, "right_factor": right_factor}


def reference(gradient, momentum, right_factor):
    whole = momentum + gradient.astype(jnp.float32)
    wide = whole.astype(jnp.bfloat16)
    left = jnp.dot(wide.astype(jnp.float32), right_factor.astype(jnp.float32), preferred_element_type=jnp.float32)
    gram = jnp.dot(left.T, left, precision=lax.Precision.HIGHEST)
    lower = jnp.linalg.cholesky(gram)
    ortho = jax.scipy.linalg.solve_triangular(lower, left.T, lower=True).T.astype(jnp.bfloat16)
    right = lax.dot_general(wide.astype(jnp.float32), ortho.astype(jnp.float32), (((0,), (0,)), ((), ())), preferred_element_type=jnp.float32)
    right_b = right.astype(jnp.bfloat16)
    right_f = right_b.astype(jnp.float32)
    norms = jnp.sqrt(lax.optimization_barrier(jnp.sum(right_f * right_f, axis=0)) + 1e-06)
    factor_new = (math.sqrt(FFW) * right_f / norms).astype(jnp.bfloat16)
    scaled = (ortho.astype(jnp.float32) * (norms / math.sqrt(FFW))).astype(jnp.bfloat16)
    dims = (((1,), (1,)), ((), ()))
    product = lax.dot_general(ortho.astype(jnp.float32), factor_new.astype(jnp.float32), dims, preferred_element_type=jnp.float32)
    update = (math.sqrt(D / RANK) * product).astype(jnp.bfloat16)
    feedback = lax.dot_general(scaled.astype(jnp.float32), factor_new.astype(jnp.float32), dims, preferred_element_type=jnp.float32)
    momentum_new = whole - 0.05 * feedback
    return (update, momentum_new, factor_new)
```

```python
import functools
import math

import jax
import jax.numpy as jnp
from jax import lax
from jax.experimental import pallas as pl
from jax.experimental.pallas import tpu as pltpu
from jax.sharding import PartitionSpec as P

D = 8192
FFW = 14336
RANK = 512
N = 8
ROWS = 28
PAD = 32
HALF = 16
PARTS = 2
WIDTH = N // PARTS
MESH = pl.DeviceIdType.MESH
HIGHEST = lax.Precision.HIGHEST
VMEM = pl.BlockSpec(memory_space=pltpu.VMEM)


def params(collective_id):
    return pltpu.CompilerParams(
        collective_id=collective_id, has_side_effects=True, vmem_limit_bytes=48 * 2**20
    )


def wrap(index):
    return lax.rem(index + 2 * N, N)


def greet(peers):
    barrier = pltpu.get_barrier_semaphore()
    for peer in peers:
        pl.semaphore_signal(barrier, inc=1, device_id=peer, device_id_type=MESH)
    pl.semaphore_wait(barrier, len(peers))


def remote(src, dst, send_sem, recv_sem, device):
    return pltpu.make_async_remote_copy(
        src_ref=src, dst_ref=dst, send_sem=send_sem, recv_sem=recv_sem,
        device_id=device, device_id_type=MESH,
    )


def place():
    fsdp = lax.axis_index("fsdp")
    return fsdp // N, lax.rem(fsdp, N), lax.axis_index("tp")


def line_device(axis, offset):
    y, z, tp = place()
    if axis == 0:
        return (wrap(y + offset) * N + z, tp)
    return (y * N + wrap(z + offset), tp)


def plane_peers():
    return [line_device(axis, k) for axis in range(2) for k in range(1, N)]


def chain_length(direction, part):
    return N // 2 if direction == part else N // 2 - 1


CHAINS = [(h, d, p) for h in range(2) for d in range(2) for p in range(PARTS)]


def gather_plane(x_ref, out_ref, sems):
    send1, recv1, send2, recv2 = sems
    y, z, _ = place()
    ring = (y, z)
    sends = []
    for k in range(1, N):
        for h in range(2):
            rows = pl.ds(h * HALF, HALF)
            copy = remote(
                x_ref.at[rows], out_ref.at[y, z, rows],
                send1.at[h, k], recv1.at[h, k], line_device(1 - h, k),
            )
            copy.start()
            sends.append(copy)
    out_ref[y, z] = x_ref[...]
    for copy in sends:
        copy.wait_recv()

    def slot(h, index, part):
        part = pl.ds(part * WIDTH, WIDTH)
        rows = pl.ds(h * HALF, HALF)
        return out_ref.at[index, part, rows] if h == 0 else out_ref.at[part, index, rows]

    arriving = {}
    for step in range(1, N // 2 + 2):
        for h, d, p in CHAINS:
            sign = 1 - 2 * d
            if (h, d, p, step - 1) in arriving:
                arriving[h, d, p, step - 1].wait_recv()
            if step <= chain_length(d, p):
                ref = slot(h, wrap(ring[h] - sign * (step - 1)), p)
                copy = remote(
                    ref, ref, send2.at[h, d, step, p], recv2.at[h, d, step, p],
                    line_device(h, sign),
                )
                copy.start()
                sends.append(copy)
                arriving[h, d, p, step] = copy
    for copy in sends:
        copy.wait_send()


GATHER_SEMS = [
    pltpu.SemaphoreType.DMA((2, N)),
    pltpu.SemaphoreType.DMA((2, N)),
    pltpu.SemaphoreType.DMA((2, 2, N // 2 + 1, PARTS)),
    pltpu.SemaphoreType.DMA((2, 2, N // 2 + 1, PARTS)),
]


def gather_kernel(x_ref, out_ref, *sems):
    greet(plane_peers())
    gather_plane(x_ref, out_ref, sems)


def gather(x):
    return pl.pallas_call(
        gather_kernel,
        out_shape=jax.ShapeDtypeStruct((N, N, PAD, RANK), jnp.bfloat16),
        in_specs=[VMEM],
        out_specs=VMEM,
        scratch_shapes=list(GATHER_SEMS),
        compiler_params=params(0),
        name="gather_factor",
    )(x)


def tp_device(offset):
    return (lax.axis_index("fsdp"), wrap(lax.axis_index("tp") + offset))


def left_kernel(x_ref, out_ref, landed, send1, recv1, send2, recv2):
    tp = lax.axis_index("tp")
    greet([tp_device(k) for k in range(1, N)])

    def rows(index):
        return pl.ds(pl.multiple_of(index * HALF, HALF), HALF)

    copies = []
    for k in range(1, N):
        copy = remote(
            x_ref.at[rows(wrap(tp + k))], landed.at[k], send1.at[k], recv1.at[k], tp_device(k)
        )
        copy.start()
        copies.append(copy)
    total = x_ref[rows(tp), :]
    for k, copy in enumerate(copies):
        copy.wait_recv()
        total = total + landed[k + 1]
    out_ref[rows(tp), :] = total
    second = []
    for k in range(1, N):
        copy = remote(
            out_ref.at[rows(tp)], out_ref.at[rows(tp)], send2.at[k], recv2.at[k], tp_device(k)
        )
        copy.start()
        second.append(copy)
    for copy in second:
        copy.wait_recv()
    for copy in copies + second:
        copy.wait_send()


def sum_left(partial_value):
    return pl.pallas_call(
        left_kernel,
        out_shape=jax.ShapeDtypeStruct(partial_value.shape, jnp.float32),
        in_specs=[VMEM],
        out_specs=VMEM,
        scratch_shapes=[pltpu.VMEM((N, HALF, RANK), jnp.float32)]
        + [pltpu.SemaphoreType.DMA((N,)) for _ in range(4)],
        compiler_params=params(1),
        name="sum_left",
    )(partial_value)


def gram_kernel(gram_ref, out_ref, landed1, landed2, mine, send1, recv1, send2, recv2, send3, recv3):
    y, z, tp = place()
    greet(plane_peers())
    copies = []
    for k in range(1, N):
        row = pl.multiple_of(tp * (RANK // N) + wrap(z + k) * N, N)
        copy = remote(
            gram_ref.at[pl.ds(row, N)], landed1.at[k], send1.at[k], recv1.at[k], line_device(1, k)
        )
        copy.start()
        copies.append(copy)
    total = gram_ref[pl.ds(pl.multiple_of(tp * (RANK // N) + z * N, N), N), :]
    for k, copy in enumerate(copies):
        copy.wait_recv()
        total = total + landed1[k + 1]
    landed2[y] = total
    mine[...] = total
    second = []
    for k in range(1, N):
        copy = remote(mine, landed2.at[y], send2.at[k], recv2.at[k], line_device(0, k))
        copy.start()
        second.append(copy)
    for copy in second:
        copy.wait_recv()
    total = landed2[0]
    for k in range(1, N):
        total = total + landed2[k]
    rows = pl.ds(pl.multiple_of(z * N, N), N)
    out_ref[rows, :] = total
    third = []
    for k in range(1, N):
        copy = remote(out_ref.at[rows], out_ref.at[rows], send3.at[k], recv3.at[k], line_device(1, k))
        copy.start()
        third.append(copy)
    for copy in third:
        copy.wait_recv()
    for copy in copies + second + third:
        copy.wait_send()


def sum_gram(gram):
    return pl.pallas_call(
        gram_kernel,
        out_shape=jax.ShapeDtypeStruct((RANK // N, RANK), jnp.float32),
        in_specs=[VMEM],
        out_specs=VMEM,
        scratch_shapes=[
            pltpu.VMEM((N, N, RANK), jnp.float32),
            pltpu.VMEM((N, N, RANK), jnp.float32),
            pltpu.VMEM((N, RANK), jnp.float32),
        ]
        + [pltpu.SemaphoreType.DMA((N,)) for _ in range(6)],
        compiler_params=params(2),
        name="sum_gram",
    )(gram)


def spread_kernel(x_ref, out_ref, send1, recv1, send2, recv2):
    tp = lax.axis_index("tp")
    fsdp = lax.axis_index("fsdp")
    size = RANK // N
    sibling = (fsdp, tp + 1 - 2 * lax.rem(tp, 2))
    greet([tp_device(2), tp_device(4), tp_device(6), sibling])

    def rows(index):
        return pl.ds(pl.multiple_of(index * size, size), size)

    copies = []
    for k in range(1, N // 2):
        copy = remote(
            x_ref, out_ref.at[rows(tp)], send1.at[k], recv1.at[k], tp_device(2 * k)
        )
        copy.start()
        copies.append(copy)
    near = [remote(x_ref, out_ref.at[rows(tp)], send2.at[0], recv2.at[0], sibling)]
    near[0].start()
    out_ref[rows(tp), :] = x_ref[...]
    for k in (1, 3, 2):
        copies[k - 1].wait_recv()
        ref = out_ref.at[rows(wrap(tp - 2 * k))]
        copy = remote(ref, ref, send2.at[k], recv2.at[k], sibling)
        copy.start()
        near.append(copy)
    for copy in near:
        copy.wait_recv()
    for copy in copies + near:
        copy.wait_send()


def spread_gram(x):
    return pl.pallas_call(
        spread_kernel,
        out_shape=jax.ShapeDtypeStruct((RANK, RANK), jnp.float32),
        in_specs=[VMEM],
        out_specs=VMEM,
        scratch_shapes=[pltpu.SemaphoreType.DMA((N // 2,)) for _ in range(4)],
        compiler_params=params(3),
        name="spread_gram",
    )(x)


BLOCK = 128
BASE = 8


def small_inverse(panel, first):
    wide = (BASE, BLOCK)
    entry = {
        (i, j): jnp.broadcast_to(panel[i : i + 1, first + j : first + j + 1], wide)
        for i in range(BASE)
        for j in range(i + 1)
    }
    lower, inverse, scale = {}, {}, {}
    for j in range(BASE):
        pivot = entry[j, j]
        guess = lax.rsqrt(pivot)
        scale[j] = guess * (1.5 - 0.5 * ((pivot * guess) * guess))
        for i in range(j + 1, BASE):
            lower[i, j] = entry[i, j] * scale[j]
        for i in range(j + 1, BASE):
            for m in range(j + 1, i + 1):
                entry[i, m] = entry[i, m] - lower[i, j] * lower[m, j]
    for j in range(BASE):
        inverse[j, j] = scale[j]
        for i in range(j + 1, BASE):
            total = lower[i, j] * inverse[j, j]
            for m in range(j + 1, i):
                total = total + lower[i, m] * inverse[m, j]
            inverse[i, j] = -(scale[i] * total)
    index = lax.broadcasted_iota(jnp.int32, wide, 0)
    columns, rows = [], []
    for j in range(BASE):
        column = jnp.zeros(wide, jnp.float32)
        row = jnp.zeros(wide, jnp.float32)
        for i in range(j, BASE):
            column = jnp.where(index == i, inverse[i, j], column)
        for i in range(j + 1):
            row = jnp.where(index == i, inverse[j, i], row)
        columns.append(column)
        rows.append(row)
    return columns, rows


def combine(factors, panel):
    pieces = []
    for start in range(0, panel.shape[1], BLOCK):
        piece = panel[:, start : start + BLOCK]
        total = factors[0] * piece[0:1, :]
        for m in range(1, BASE):
            total = total + factors[m] * piece[m : m + 1, :]
        pieces.append(total)
    return jnp.concatenate(pieces, axis=1)


def ortho_kernel(gram_ref, left_ref, out_ref, rest, work, tail):
    rest[...] = gram_ref[...]
    tail[...] = left_ref[...]
    row = lax.broadcasted_iota(jnp.int32, (BLOCK, BLOCK), 0)
    column = lax.broadcasted_iota(jnp.int32, (BLOCK, BLOCK), 1)

    def block_step(k, carry):
        at = pl.ds(pl.multiple_of(k * BLOCK, BLOCK), BLOCK)
        work[:, :BLOCK] = rest[at, at]
        work[:, BLOCK:] = jnp.where(row == column, 1.0, 0.0).astype(jnp.float32)
        for first in range(0, BLOCK, BASE):
            panel = work[first : first + BASE, :]
            columns, rows = small_inverse(panel, first)
            solved = combine(columns, panel)
            work[first : first + BASE, :] = solved
            after = first + BASE
            if after < BLOCK:
                again = combine(rows, solved)
                parts = [again, jnp.zeros((BLOCK - after, 2 * BLOCK), jnp.float32)]
                if first:
                    parts = [jnp.zeros((first, 2 * BLOCK), jnp.float32)] + parts
                work[after:, :] = work[after:, :] - jnp.dot(
                    work[after:, :BLOCK], jnp.concatenate(parts, axis=0), precision=HIGHEST,
                    preferred_element_type=jnp.float32,
                )
        inverse = jnp.where(row >= column, work[:, BLOCK:], 0.0)
        panel = jnp.dot(inverse, rest[at, :], precision=HIGHEST, preferred_element_type=jnp.float32)
        lanes = lax.broadcasted_iota(jnp.int32, (BLOCK, RANK), 1)
        panel = jnp.where(lanes >= (k + 1) * BLOCK, panel, 0.0)
        rest[...] = rest[...] - lax.dot_general(
            panel, panel, (((0,), (0,)), ((), ())), precision=HIGHEST,
            preferred_element_type=jnp.float32,
        )
        done = lax.dot_general(
            tail[:, at], inverse, (((1,), (1,)), ((), ())), precision=HIGHEST,
            preferred_element_type=jnp.float32,
        )
        out_ref[:, at] = done.astype(out_ref.dtype)
        tail[...] = tail[...] - jnp.dot(
            done, panel, precision=HIGHEST, preferred_element_type=jnp.float32
        )
        return carry

    lax.fori_loop(0, RANK // BLOCK, block_step, 0)


def orthonormalize(gram, left):
    return pl.pallas_call(
        ortho_kernel,
        out_shape=jax.ShapeDtypeStruct(left.shape, jnp.bfloat16),
        in_specs=[VMEM, VMEM],
        out_specs=VMEM,
        scratch_shapes=[
            pltpu.VMEM((RANK, RANK), jnp.float32),
            pltpu.VMEM((BLOCK, 2 * BLOCK), jnp.float32),
            pltpu.VMEM(left.shape, jnp.float32),
        ],
        compiler_params=pltpu.CompilerParams(vmem_limit_bytes=48 * 2**20),
        name="orthonormalize",
    )(gram, left)


def right_kernel(
    wide_ref, ortho_ref, mine_ref, out_ref, chain, summed, landed,
    send1, recv1, send2, recv2, *gather_sems,
):
    y, z, _ = place()
    ring = (y, z)
    greet(plane_peers())

    def own(h, target, part):
        target = wrap(target)
        part = pl.ds(part * WIDTH, WIDTH)
        rows = pl.ds(h * HALF, HALF)
        block = wide_ref[target, part, rows] if h == 0 else wide_ref[part, target, rows]
        block = block.reshape(WIDTH * HALF, block.shape[-1])
        product = jnp.dot(block, ortho_ref[...], preferred_element_type=jnp.float32)
        return product.reshape(WIDTH, HALF, RANK)

    sends, arriving = [], {}

    def pass_on(h, d, p, step):
        copy = remote(
            chain.at[h, d, step - 1, p], chain.at[h, d, step, p],
            send1.at[h, d, step, p], recv1.at[h, d, step, p], line_device(h, 1 - 2 * d),
        )
        copy.start()
        sends.append(copy)
        arriving[h, d, p, step] = copy

    for h, d, p in CHAINS:
        length = chain_length(d, p)
        chain[h, d, 0, p] = own(h, ring[h] + (1 - 2 * d) * length, p).astype(jnp.bfloat16)
        pass_on(h, d, p, 1)
    for step in range(1, N // 2):
        for h, d, p in CHAINS:
            length = chain_length(d, p)
            if step < length:
                term = own(h, ring[h] + (1 - 2 * d) * (length - step), p)
                arriving[h, d, p, step].wait_recv()
                term = term + chain[h, d, step, p].astype(jnp.float32)
                chain[h, d, step, p] = term.astype(jnp.bfloat16)
                pass_on(h, d, p, step + 1)
    for h in range(2):
        for p in range(PARTS):
            term = own(h, ring[h], p)
            for d in range(2):
                length = chain_length(d, p)
                arriving[h, d, p, length].wait_recv()
                term = term + chain[h, d, length, p].astype(jnp.float32)
            summed[h, p * WIDTH : (p + 1) * WIDTH] = term
    second = {}
    for h in range(2):
        for k in range(1, N):
            copy = remote(
                summed.at[h, wrap(ring[1 - h] + k)], landed.at[h, k],
                send2.at[h, k], recv2.at[h, k], line_device(1 - h, k),
            )
            copy.start()
            sends.append(copy)
            second[h, k] = copy
    for h in range(2):
        total = summed[h, ring[1 - h]]
        for k in range(1, N):
            second[h, k].wait_recv()
            total = total + landed[h, k]
        mine_ref[pl.ds(h * HALF, HALF), :] = total.astype(jnp.bfloat16)
    gather_plane(mine_ref, out_ref, gather_sems)
    for copy in sends:
        copy.wait_send()


def sum_right(wide, ortho):
    return pl.pallas_call(
        right_kernel,
        out_shape=(
            jax.ShapeDtypeStruct((PAD, RANK), jnp.bfloat16),
            jax.ShapeDtypeStruct((N, N, PAD, RANK), jnp.bfloat16),
        ),
        in_specs=[VMEM, VMEM],
        out_specs=(VMEM, VMEM),
        scratch_shapes=[
            pltpu.VMEM((2, 2, N // 2 + 1, PARTS, WIDTH, HALF, RANK), jnp.bfloat16),
            pltpu.VMEM((2, N, HALF, RANK), jnp.float32),
            pltpu.VMEM((2, N, HALF, RANK), jnp.float32),
            pltpu.SemaphoreType.DMA((2, 2, N // 2 + 1, PARTS)),
            pltpu.SemaphoreType.DMA((2, 2, N // 2 + 1, PARTS)),
            pltpu.SemaphoreType.DMA((2, N)),
            pltpu.SemaphoreType.DMA((2, N)),
        ]
        + list(GATHER_SEMS),
        compiler_params=params(4),
        name="sum_right",
    )(wide, ortho)


def squares_kernel(x_ref, out_ref, landed, send, recv):
    tp = lax.axis_index("tp")
    greet([tp_device(k) for k in range(1, N)])
    copies = []
    for k in range(1, N):
        copy = remote(x_ref, landed.at[tp], send.at[k], recv.at[k], tp_device(k))
        copy.start()
        copies.append(copy)
    landed[tp] = x_ref[...]
    for copy in copies:
        copy.wait_recv()
    total = landed[0]
    for k in range(1, N):
        total = total + landed[k]
    out_ref[...] = total
    for copy in copies:
        copy.wait_send()


def sum_squares(x):
    return pl.pallas_call(
        squares_kernel,
        out_shape=jax.ShapeDtypeStruct(x.shape, jnp.float32),
        in_specs=[VMEM],
        out_specs=VMEM,
        scratch_shapes=[
            pltpu.VMEM((N,) + x.shape, jnp.float32),
            pltpu.SemaphoreType.DMA((N,)),
            pltpu.SemaphoreType.DMA((N,)),
        ],
        compiler_params=params(5),
        name="sum_squares",
    )(x)


def body(gradient, momentum, right_factor):
    whole = momentum + gradient.astype(jnp.float32)
    wide = whole.astype(jnp.bfloat16)
    row_count, columns = wide.shape
    blocks = wide.T.reshape(N * N, ROWS, row_count)
    blocks = jnp.pad(blocks, ((0, 0), (0, PAD - ROWS), (0, 0)))
    factor = gather(jnp.pad(right_factor, ((0, PAD - ROWS), (0, 0))))
    partial_value = lax.dot_general(
        blocks.reshape(N * N * PAD, row_count), factor.reshape(N * N * PAD, RANK),
        (((0,), (0,)), ((), ())), preferred_element_type=jnp.float32,
    )
    left = sum_left(partial_value)
    gram = spread_gram(sum_gram(jnp.dot(left.T, left, precision=HIGHEST)))
    ortho = orthonormalize(gram, left)
    mine, right = sum_right(blocks.reshape(N, N, PAD, row_count), ortho)
    right_f = right[:, :, :ROWS].reshape(columns, RANK).astype(jnp.float32)
    squares = jnp.sum((right_f * right_f).reshape(columns // N, N, RANK), axis=0)
    squares = jnp.sum(sum_squares(squares), axis=0)
    norms = jnp.sqrt(squares + 1e-06)
    factor_new = (math.sqrt(FFW) * mine[:ROWS].astype(jnp.float32) / norms).astype(jnp.bfloat16)
    factor_all = (math.sqrt(FFW) * right_f / norms).astype(jnp.bfloat16)
    scaled = (ortho.astype(jnp.float32) * (norms / math.sqrt(FFW))).astype(jnp.bfloat16)
    combined = lax.dot_general(
        jnp.concatenate([ortho, scaled], axis=0), factor_all,
        (((1,), (1,)), ((), ())), preferred_element_type=jnp.float32,
    )
    update = (math.sqrt(D / RANK) * combined[:row_count]).astype(jnp.bfloat16)
    momentum_new = whole - 0.05 * combined[row_count:]
    return (update, momentum_new, factor_new)


def solution(mesh):
    return jax.shard_map(
        body,
        mesh=mesh,
        in_specs=(P("fsdp", "tp"), P("fsdp", "tp"), P(("tp", "fsdp"), None)),
        out_specs=(P("fsdp", "tp"), P("fsdp", "tp"), P(("tp", "fsdp"), None)),
        check_vma=False,
    )
```

```python
import functools
import math

import jax
import jax.numpy as jnp
from jax import lax
from jax.experimental import pallas as pl
from jax.experimental.pallas import tpu as pltpu
from jax.sharding import PartitionSpec as P

D = 8192
FFW = 14336
RANK = 512
N = 8
ROWS = 28
PAD = 32
HALF = 16
PARTS = 2
WIDTH = N // PARTS
MESH = pl.DeviceIdType.MESH
HIGHEST = lax.Precision.HIGHEST
VMEM = pl.BlockSpec(memory_space=pltpu.VMEM)


def params(collective_id):
    return pltpu.CompilerParams(
        collective_id=collective_id, has_side_effects=True, vmem_limit_bytes=48 * 2**20
    )


def wrap(index):
    return lax.rem(index + 2 * N, N)


def greet(peers):
    barrier = pltpu.get_barrier_semaphore()
    for peer in peers:
        pl.semaphore_signal(barrier, inc=1, device_id=peer, device_id_type=MESH)
    pl.semaphore_wait(barrier, len(peers))


def remote(src, dst, send_sem, recv_sem, device):
    return pltpu.make_async_remote_copy(
        src_ref=src, dst_ref=dst, send_sem=send_sem, recv_sem=recv_sem,
        device_id=device, device_id_type=MESH,
    )


def place():
    fsdp = lax.axis_index("fsdp")
    return fsdp // N, lax.rem(fsdp, N), lax.axis_index("tp")


def line_device(axis, offset):
    y, z, tp = place()
    if axis == 0:
        return (wrap(y + offset) * N + z, tp)
    return (y * N + wrap(z + offset), tp)


def plane_peers():
    return [line_device(axis, k) for axis in range(2) for k in range(1, N)]


def chain_length(direction, part):
    return N // 2 if direction == part else N // 2 - 1


CHAINS = [(h, d, p) for p in range(PARTS) for h in range(2) for d in range(2)]


def gather_plane(x_ref, out_ref, sems, visit=None):
    send1, recv1, send2, recv2 = sems
    y, z, _ = place()
    ring = (y, z)
    sends = []
    for k in range(1, N):
        for h in range(2):
            rows = pl.ds(h * HALF, HALF)
            copy = remote(
                x_ref.at[rows], out_ref.at[y, z, rows],
                send1.at[h, k], recv1.at[h, k], line_device(1 - h, k),
            )
            copy.start()
            sends.append(copy)
    out_ref[y, z] = x_ref[...]
    for copy in sends:
        copy.wait_recv()

    def slot(h, index, part):
        part = pl.ds(part * WIDTH, WIDTH)
        rows = pl.ds(h * HALF, HALF)
        return out_ref.at[index, part, rows] if h == 0 else out_ref.at[part, index, rows]

    arriving = {}
    for step in range(1, N // 2 + 2):
        for h, d, p in CHAINS:
            sign = 1 - 2 * d
            if (h, d, p, step - 1) in arriving:
                arriving[h, d, p, step - 1].wait_recv()
            if step <= chain_length(d, p):
                ref = slot(h, wrap(ring[h] - sign * (step - 1)), p)
                copy = remote(
                    ref, ref, send2.at[h, d, step, p], recv2.at[h, d, step, p],
                    line_device(h, sign),
                )
                copy.start()
                sends.append(copy)
                arriving[h, d, p, step] = copy
        if visit is not None:
            for h, d, p in CHAINS:
                if step <= chain_length(d, p) + 1 and (step > 1 or d == 0):
                    visit(slot(h, wrap(ring[h] - (1 - 2 * d) * (step - 1)), p))
    for copy in sends:
        copy.wait_send()


GATHER_SEMS = [
    pltpu.SemaphoreType.DMA((2, N)),
    pltpu.SemaphoreType.DMA((2, N)),
    pltpu.SemaphoreType.DMA((2, 2, N // 2 + 1, PARTS)),
    pltpu.SemaphoreType.DMA((2, 2, N // 2 + 1, PARTS)),
]


def gather_kernel(x_ref, out_ref, *sems):
    greet(plane_peers())
    gather_plane(x_ref, out_ref, sems)


def gather(x):
    return pl.pallas_call(
        gather_kernel,
        out_shape=jax.ShapeDtypeStruct((N, N, PAD, RANK), jnp.bfloat16),
        in_specs=[VMEM],
        out_specs=VMEM,
        scratch_shapes=list(GATHER_SEMS),
        compiler_params=params(0),
        name="gather_factor",
    )(x)


def tp_device(offset):
    return (lax.axis_index("fsdp"), wrap(lax.axis_index("tp") + offset))


def left_kernel(x_ref, out_ref, landed, send1, recv1, send2, recv2):
    tp = lax.axis_index("tp")
    greet([tp_device(k) for k in range(1, N)])

    def rows(index):
        return pl.ds(pl.multiple_of(index * HALF, HALF), HALF)

    copies = []
    for k in range(1, N):
        copy = remote(
            x_ref.at[rows(wrap(tp + k))], landed.at[k], send1.at[k], recv1.at[k], tp_device(k)
        )
        copy.start()
        copies.append(copy)
    total = x_ref[rows(tp), :]
    for k, copy in enumerate(copies):
        copy.wait_recv()
        total = total + landed[k + 1]
    out_ref[rows(tp), :] = total
    second = []
    for k in range(1, N):
        copy = remote(
            out_ref.at[rows(tp)], out_ref.at[rows(tp)], send2.at[k], recv2.at[k], tp_device(k)
        )
        copy.start()
        second.append(copy)
    for copy in second:
        copy.wait_recv()
    for copy in copies + second:
        copy.wait_send()


def sum_left(partial_value):
    return pl.pallas_call(
        left_kernel,
        out_shape=jax.ShapeDtypeStruct(partial_value.shape, jnp.float32),
        in_specs=[VMEM],
        out_specs=VMEM,
        scratch_shapes=[pltpu.VMEM((N, HALF, RANK), jnp.float32)]
        + [pltpu.SemaphoreType.DMA((N,)) for _ in range(4)],
        compiler_params=params(1),
        name="sum_left",
    )(partial_value)


def gram_kernel(gram_ref, out_ref, landed1, landed2, mine, send1, recv1, send2, recv2, send3, recv3):
    y, z, tp = place()
    greet(plane_peers())
    copies = []
    for k in range(1, N):
        row = pl.multiple_of(tp * (RANK // N) + wrap(z + k) * N, N)
        copy = remote(
            gram_ref.at[pl.ds(row, N)], landed1.at[k], send1.at[k], recv1.at[k], line_device(1, k)
        )
        copy.start()
        copies.append(copy)
    total = gram_ref[pl.ds(pl.multiple_of(tp * (RANK // N) + z * N, N), N), :]
    for k, copy in enumerate(copies):
        copy.wait_recv()
        total = total + landed1[k + 1]
    landed2[y] = total
    mine[...] = total
    second = []
    for k in range(1, N):
        copy = remote(mine, landed2.at[y], send2.at[k], recv2.at[k], line_device(0, k))
        copy.start()
        second.append(copy)
    for copy in second:
        copy.wait_recv()
    total = landed2[0]
    for k in range(1, N):
        total = total + landed2[k]
    rows = pl.ds(pl.multiple_of(z * N, N), N)
    out_ref[rows, :] = total
    third = []
    for k in range(1, N):
        copy = remote(out_ref.at[rows], out_ref.at[rows], send3.at[k], recv3.at[k], line_device(1, k))
        copy.start()
        third.append(copy)
    for copy in third:
        copy.wait_recv()
    for copy in copies + second + third:
        copy.wait_send()


def sum_gram(gram):
    return pl.pallas_call(
        gram_kernel,
        out_shape=jax.ShapeDtypeStruct((RANK // N, RANK), jnp.float32),
        in_specs=[VMEM],
        out_specs=VMEM,
        scratch_shapes=[
            pltpu.VMEM((N, N, RANK), jnp.float32),
            pltpu.VMEM((N, N, RANK), jnp.float32),
            pltpu.VMEM((N, RANK), jnp.float32),
        ]
        + [pltpu.SemaphoreType.DMA((N,)) for _ in range(6)],
        compiler_params=params(2),
        name="sum_gram",
    )(gram)


def spread_kernel(x_ref, out_ref, send1, recv1, send2, recv2):
    tp = lax.axis_index("tp")
    fsdp = lax.axis_index("fsdp")
    size = RANK // N
    sibling = (fsdp, tp + 1 - 2 * lax.rem(tp, 2))
    greet([tp_device(2), tp_device(4), tp_device(6), sibling])

    def rows(index):
        return pl.ds(pl.multiple_of(index * size, size), size)

    copies = []
    for k in range(1, N // 2):
        copy = remote(
            x_ref, out_ref.at[rows(tp)], send1.at[k], recv1.at[k], tp_device(2 * k)
        )
        copy.start()
        copies.append(copy)
    near = [remote(x_ref, out_ref.at[rows(tp)], send2.at[0], recv2.at[0], sibling)]
    near[0].start()
    out_ref[rows(tp), :] = x_ref[...]
    for k in (1, 3, 2):
        copies[k - 1].wait_recv()
        ref = out_ref.at[rows(wrap(tp - 2 * k))]
        copy = remote(ref, ref, send2.at[k], recv2.at[k], sibling)
        copy.start()
        near.append(copy)
    for copy in near:
        copy.wait_recv()
    for copy in copies + near:
        copy.wait_send()


def spread_gram(x):
    return pl.pallas_call(
        spread_kernel,
        out_shape=jax.ShapeDtypeStruct((RANK, RANK), jnp.float32),
        in_specs=[VMEM],
        out_specs=VMEM,
        scratch_shapes=[pltpu.SemaphoreType.DMA((N // 2,)) for _ in range(4)],
        compiler_params=params(3),
        name="spread_gram",
    )(x)


BLOCK = 128
BASE = 8


def small_inverse(panel, first):
    wide = (BASE, BLOCK)
    entry = {
        (i, j): jnp.broadcast_to(panel[i : i + 1, first + j : first + j + 1], wide)
        for i in range(BASE)
        for j in range(i + 1)
    }
    lower, inverse, scale = {}, {}, {}
    for j in range(BASE):
        pivot = entry[j, j]
        guess = lax.rsqrt(pivot)
        scale[j] = guess * (1.5 - 0.5 * ((pivot * guess) * guess))
        for i in range(j + 1, BASE):
            lower[i, j] = entry[i, j] * scale[j]
        for i in range(j + 1, BASE):
            for m in range(j + 1, i + 1):
                entry[i, m] = entry[i, m] - lower[i, j] * lower[m, j]
    for j in range(BASE):
        inverse[j, j] = scale[j]
        for i in range(j + 1, BASE):
            total = lower[i, j] * inverse[j, j]
            for m in range(j + 1, i):
                total = total + lower[i, m] * inverse[m, j]
            inverse[i, j] = -(scale[i] * total)
    index = lax.broadcasted_iota(jnp.int32, wide, 0)
    columns, rows = [], []
    for j in range(BASE):
        column = jnp.zeros(wide, jnp.float32)
        row = jnp.zeros(wide, jnp.float32)
        for i in range(j, BASE):
            column = jnp.where(index == i, inverse[i, j], column)
        for i in range(j + 1):
            row = jnp.where(index == i, inverse[j, i], row)
        columns.append(column)
        rows.append(row)
    return columns, rows


def add_up(terms):
    while len(terms) > 1:
        terms = [sum(terms[i + 1 : i + 2], terms[i]) for i in range(0, len(terms), 2)]
    return terms[0]


def combine(factors, panel):
    return [
        add_up([factors[m] * piece[m : m + 1, :] for m in range(BASE)]) for piece in panel
    ]


def block_inverse(block):
    row = lax.broadcasted_iota(jnp.int32, (BLOCK, BLOCK), 0)
    column = lax.broadcasted_iota(jnp.int32, (BLOCK, BLOCK), 1)
    unit = jnp.where(row == column, 1.0, 0.0).astype(jnp.float32)
    count = BLOCK // BASE
    panels = [
        [matrix[b * BASE : (b + 1) * BASE, :] for matrix in (block, unit)] for b in range(count)
    ]
    solved = []
    for b in range(count):
        first = b * BASE
        columns, rows = small_inverse(panels[b][0], first)
        done = combine(columns, panels[b])
        solved.append(done[1])
        if b + 1 == count:
            break
        again = combine(rows, done)
        ahead = panels[b + 1]
        factors = [
            jnp.broadcast_to(ahead[0][:, first + m : first + m + 1], (BASE, BLOCK))
            for m in range(BASE)
        ]
        panels[b + 1] = [old - new for old, new in zip(ahead, combine(factors, again))]
        if b + 2 == count:
            continue
        multiplier = jnp.concatenate([panels[c][0] for c in range(b + 2, count)], axis=0)
        parts = [jnp.concatenate(again, axis=1)]
        parts.append(jnp.zeros((BLOCK - first - BASE, 2 * BLOCK), jnp.float32))
        if first:
            parts.insert(0, jnp.zeros((first, 2 * BLOCK), jnp.float32))
        change = jnp.dot(
            multiplier, jnp.concatenate(parts, axis=0), precision=HIGHEST,
            preferred_element_type=jnp.float32,
        )
        for c in range(b + 2, count):
            at = (c - b - 2) * BASE
            panels[c] = [
                old - change[at : at + BASE, i * BLOCK : (i + 1) * BLOCK]
                for i, old in enumerate(panels[c])
            ]
    return jnp.where(row >= column, jnp.concatenate(solved, axis=0), 0.0)


def full_dot(x, y, dims):
    return lax.dot_general(
        x, y, (dims, ((), ())), precision=HIGHEST, preferred_element_type=jnp.float32
    )


def ortho_kernel(gram_ref, left_ref, out_ref, rest, tail):
    rest[...] = gram_ref[...]
    tail[...] = left_ref[...]
    for at in range(0, RANK, BLOCK):
        end = at + BLOCK
        inverse = block_inverse(rest[at:end, at:end])
        done = full_dot(tail[:, at:end], inverse, ((1,), (1,)))
        out_ref[:, at:end] = done.astype(out_ref.dtype)
        if end == RANK:
            break
        panel = full_dot(inverse, rest[at:end, end:], ((1,), (0,)))
        for start in range(end, RANK, BLOCK):
            piece = panel[:, start - end : start - end + BLOCK]
            rest[start : start + BLOCK, start:] -= full_dot(
                piece, panel[:, start - end :], ((0,), (0,))
            )
        tail[:, end:] -= full_dot(done, panel, ((1,), (0,)))


def orthonormalize(gram, left):
    return pl.pallas_call(
        ortho_kernel,
        out_shape=jax.ShapeDtypeStruct(left.shape, jnp.bfloat16),
        in_specs=[VMEM, VMEM],
        out_specs=VMEM,
        scratch_shapes=[
            pltpu.VMEM((RANK, RANK), jnp.float32),
            pltpu.VMEM(left.shape, jnp.float32),
        ],
        compiler_params=pltpu.CompilerParams(vmem_limit_bytes=48 * 2**20),
        name="orthonormalize",
    )(gram, left)


def right_kernel(
    wide_ref, ortho_ref, mine_ref, out_ref, squares_ref, chain, summed, landed,
    send1, recv1, send2, recv2, *gather_sems,
):
    y, z, _ = place()
    ring = (y, z)
    greet(plane_peers())

    def own(h, target, part):
        target = wrap(target)
        part = pl.ds(part * WIDTH, WIDTH)
        rows = pl.ds(h * HALF, HALF)
        block = wide_ref[target, part, rows] if h == 0 else wide_ref[part, target, rows]
        block = block.reshape(WIDTH * HALF, block.shape[-1])
        product = jnp.dot(block, ortho_ref[...], preferred_element_type=jnp.float32)
        return product.reshape(WIDTH, HALF, RANK)

    sends, arriving = [], {}

    def pass_on(h, d, p, step):
        copy = remote(
            chain.at[h, d, step - 1, p], chain.at[h, d, step, p],
            send1.at[h, d, step, p], recv1.at[h, d, step, p], line_device(h, 1 - 2 * d),
        )
        copy.start()
        sends.append(copy)
        arriving[h, d, p, step] = copy

    for h, d, p in CHAINS:
        length = chain_length(d, p)
        chain[h, d, 0, p] = own(h, ring[h] + (1 - 2 * d) * length, p).astype(jnp.bfloat16)
        pass_on(h, d, p, 1)
    for step in range(1, N // 2):
        for h, d, p in CHAINS:
            length = chain_length(d, p)
            if step < length:
                term = own(h, ring[h] + (1 - 2 * d) * (length - step), p)
                arriving[h, d, p, step].wait_recv()
                term = term + chain[h, d, step, p].astype(jnp.float32)
                chain[h, d, step, p] = term.astype(jnp.bfloat16)
                pass_on(h, d, p, step + 1)
    for h in range(2):
        for p in range(PARTS):
            term = own(h, ring[h], p)
            for d in range(2):
                length = chain_length(d, p)
                arriving[h, d, p, length].wait_recv()
                term = term + chain[h, d, length, p].astype(jnp.float32)
            summed[h, p * WIDTH : (p + 1) * WIDTH] = term.astype(jnp.bfloat16)
    second = {}
    for h in range(2):
        for k in range(1, N):
            copy = remote(
                summed.at[h, wrap(ring[1 - h] + k)], landed.at[h, k],
                send2.at[h, k], recv2.at[h, k], line_device(1 - h, k),
            )
            copy.start()
            sends.append(copy)
            second[h, k] = copy
    for h in range(2):
        total = summed[h, ring[1 - h]].astype(jnp.float32)
        for k in range(1, N):
            second[h, k].wait_recv()
            total = total + landed[h, k].astype(jnp.float32)
        mine_ref[pl.ds(h * HALF, HALF), :] = total.astype(jnp.bfloat16)
    squares_ref[...] = jnp.zeros_like(squares_ref)

    def add_squares(ref):
        block = ref[...].astype(jnp.float32).reshape(WIDTH * HALF // N, N, RANK)
        squares_ref[...] += jnp.sum(block * block, axis=0)

    gather_plane(mine_ref, out_ref, gather_sems, add_squares)
    for copy in sends:
        copy.wait_send()


def sum_right(wide, ortho):
    return pl.pallas_call(
        right_kernel,
        out_shape=(
            jax.ShapeDtypeStruct((PAD, RANK), jnp.bfloat16),
            jax.ShapeDtypeStruct((N, N, PAD, RANK), jnp.bfloat16),
            jax.ShapeDtypeStruct((N, RANK), jnp.float32),
        ),
        in_specs=[VMEM, VMEM],
        out_specs=(VMEM, VMEM, VMEM),
        scratch_shapes=[
            pltpu.VMEM((2, 2, N // 2 + 1, PARTS, WIDTH, HALF, RANK), jnp.bfloat16),
            pltpu.VMEM((2, N, HALF, RANK), jnp.bfloat16),
            pltpu.VMEM((2, N, HALF, RANK), jnp.bfloat16),
            pltpu.SemaphoreType.DMA((2, 2, N // 2 + 1, PARTS)),
            pltpu.SemaphoreType.DMA((2, 2, N // 2 + 1, PARTS)),
            pltpu.SemaphoreType.DMA((2, N)),
            pltpu.SemaphoreType.DMA((2, N)),
        ]
        + list(GATHER_SEMS),
        compiler_params=params(4),
        name="sum_right",
    )(wide, ortho)


def squares_kernel(x_ref, out_ref, landed, send, recv):
    tp = lax.axis_index("tp")
    greet([tp_device(k) for k in range(1, N)])
    copies = []
    for k in range(1, N):
        copy = remote(x_ref, landed.at[tp], send.at[k], recv.at[k], tp_device(k))
        copy.start()
        copies.append(copy)
    landed[tp] = x_ref[...]
    for copy in copies:
        copy.wait_recv()
    total = landed[0]
    for k in range(1, N):
        total = total + landed[k]
    out_ref[...] = total
    for copy in copies:
        copy.wait_send()


def sum_squares(x):
    return pl.pallas_call(
        squares_kernel,
        out_shape=jax.ShapeDtypeStruct(x.shape, jnp.float32),
        in_specs=[VMEM],
        out_specs=VMEM,
        scratch_shapes=[
            pltpu.VMEM((N,) + x.shape, jnp.float32),
            pltpu.SemaphoreType.DMA((N,)),
            pltpu.SemaphoreType.DMA((N,)),
        ],
        compiler_params=params(5),
        name="sum_squares",
    )(x)


def finish_kernel(
    squares_ref, right_ref, mine_ref, ortho_ref, gradient_ref, momentum_ref,
    update_ref, new_ref, factor_ref, factor,
):
    squares = jnp.sum(squares_ref[...], axis=0, keepdims=True)
    norms = jnp.sqrt(squares + 1e-06)
    gain = math.sqrt(FFW) / norms
    factor_ref[...] = (mine_ref[...].astype(jnp.float32) * gain)[:ROWS].astype(jnp.bfloat16)
    ortho = ortho_ref[...]
    scaled = (ortho.astype(jnp.float32) * (norms / math.sqrt(FFW))).astype(jnp.bfloat16)
    stacked = jnp.concatenate([ortho, scaled], axis=0)
    group = 4
    for first in range(0, right_ref.shape[0], group):
        pieces = [
            (right_ref[first + i].astype(jnp.float32) * gain)[:ROWS] for i in range(group)
        ]
        factor[first * ROWS : (first + group) * ROWS, :] = jnp.concatenate(
            pieces, axis=0
        ).astype(jnp.bfloat16)
    combined = lax.dot_general(
        stacked, factor[...], (((1,), (1,)), ((), ())), preferred_element_type=jnp.float32
    )
    rows = ortho.shape[0]
    update_ref[...] = (math.sqrt(D / RANK) * combined[:rows]).astype(jnp.bfloat16)
    whole = momentum_ref[...] + gradient_ref[...].astype(jnp.float32)
    new_ref[...] = whole - 0.05 * combined[rows:]


def finish(squares, right, mine, ortho, gradient, momentum):
    steps = 2
    rows, columns = gradient.shape
    blocks = N * N // steps
    whole = lambda shape: pl.BlockSpec(shape, lambda i: (0, 0))
    tile = pl.BlockSpec((rows, columns // steps), lambda i: (0, i))
    return pl.pallas_call(
        finish_kernel,
        grid=(steps,),
        out_shape=(
            jax.ShapeDtypeStruct((rows, columns), jnp.bfloat16),
            jax.ShapeDtypeStruct((rows, columns), jnp.float32),
            jax.ShapeDtypeStruct((ROWS, RANK), jnp.bfloat16),
        ),
        in_specs=[
            whole((N, RANK)),
            pl.BlockSpec((blocks, PAD, RANK), lambda i: (i, 0, 0)),
            whole((PAD, RANK)),
            whole((rows, RANK)),
            tile,
            tile,
        ],
        out_specs=(tile, tile, whole((ROWS, RANK))),
        scratch_shapes=[pltpu.VMEM((blocks * ROWS, RANK), jnp.bfloat16)],
        compiler_params=pltpu.CompilerParams(vmem_limit_bytes=48 * 2**20),
        name="finish",
    )(squares, right, mine, ortho, gradient, momentum)


def body(gradient, momentum, right_factor):
    wide = (momentum + gradient.astype(jnp.float32)).astype(jnp.bfloat16)
    row_count = wide.shape[0]
    blocks = wide.T.reshape(N * N, ROWS, row_count)
    blocks = jnp.pad(blocks, ((0, 0), (0, PAD - ROWS), (0, 0)))
    factor = gather(jnp.pad(right_factor, ((0, PAD - ROWS), (0, 0))))
    partial_value = lax.dot_general(
        blocks.reshape(N * N * PAD, row_count), factor.reshape(N * N * PAD, RANK),
        (((0,), (0,)), ((), ())), preferred_element_type=jnp.float32,
    )
    left = sum_left(partial_value)
    gram = spread_gram(sum_gram(jnp.dot(left.T, left, precision=HIGHEST)))
    ortho = orthonormalize(gram, left)
    mine, right, squares = sum_right(blocks.reshape(N, N, PAD, row_count), ortho)
    right = right.reshape(N * N, PAD, RANK)
    return finish(sum_squares(squares), right, mine, ortho, gradient, momentum)


def solution(mesh):
    return jax.shard_map(
        body,
        mesh=mesh,
        in_specs=(P("fsdp", "tp"), P("fsdp", "tp"), P(("tp", "fsdp"), None)),
        out_specs=(P("fsdp", "tp"), P("fsdp", "tp"), P(("tp", "fsdp"), None)),
        check_vma=False,
    )
```

```python
import functools
import math

import jax
import jax.numpy as jnp
from jax import lax
from jax.experimental import pallas as pl
from jax.experimental.pallas import tpu as pltpu
from jax.sharding import PartitionSpec as P

D = 8192
FFW = 14336
RANK = 512
N = 8
ROWS = 28
PAD = 32
HALF = 16
PARTS = 2
WIDTH = N // PARTS
MESH = pl.DeviceIdType.MESH
HIGHEST = lax.Precision.HIGHEST
VMEM = pl.BlockSpec(memory_space=pltpu.VMEM)


def params(collective_id):
    return pltpu.CompilerParams(
        collective_id=collective_id, has_side_effects=True, vmem_limit_bytes=48 * 2**20
    )


def wrap(index):
    return lax.rem(index + 2 * N, N)


def greet(peers):
    barrier = pltpu.get_barrier_semaphore()
    for peer in peers:
        pl.semaphore_signal(barrier, inc=1, device_id=peer, device_id_type=MESH)
    pl.semaphore_wait(barrier, len(peers))


def remote(src, dst, send_sem, recv_sem, device):
    return pltpu.make_async_remote_copy(
        src_ref=src, dst_ref=dst, send_sem=send_sem, recv_sem=recv_sem,
        device_id=device, device_id_type=MESH,
    )


def place():
    fsdp = lax.axis_index("fsdp")
    return fsdp // N, lax.rem(fsdp, N), lax.axis_index("tp")


def line_device(axis, offset):
    y, z, tp = place()
    if axis == 0:
        return (wrap(y + offset) * N + z, tp)
    return (y * N + wrap(z + offset), tp)


def tp_device(offset):
    return (lax.axis_index("fsdp"), wrap(lax.axis_index("tp") + offset))


def all_peers():
    plane = [line_device(axis, k) for axis in range(2) for k in range(1, N)]
    return plane + [tp_device(k) for k in range(1, N)]


def chain_length(direction, part):
    return N // 2 if direction == part else N // 2 - 1


CHAINS = [(h, d, p) for p in range(PARTS) for h in range(2) for d in range(2)]
CHAIN_SEMS = (2, 2, N // 2, PARTS)


def gather_plane(mine, out, sems, visit, sends):
    send1, recv1, send2, recv2 = sems
    y, z, _ = place()
    ring, across = (y, z), (z, y)
    direct = []
    for k in range(1, N):
        for h in range(2):
            copy = remote(
                mine.at[h], out.at[h, ring[h], across[h]],
                send1.at[h, k - 1], recv1.at[h, k - 1], line_device(1 - h, k),
            )
            copy.start()
            direct.append(copy)
    for h in range(2):
        out[h, ring[h], across[h]] = mine[h]
    yield
    for copy in direct:
        copy.wait_recv()
    sends += direct
    arriving = {}
    for step in range(1, N // 2 + 2):
        for h, d, p in CHAINS:
            sign = 1 - 2 * d
            if (h, d, p, step - 1) in arriving:
                arriving[h, d, p, step - 1].wait_recv()
            if step <= chain_length(d, p):
                ref = out.at[h, wrap(ring[h] - sign * (step - 1)), pl.ds(p * WIDTH, WIDTH)]
                copy = remote(
                    ref, ref, send2.at[h, d, step - 1, p], recv2.at[h, d, step - 1, p],
                    line_device(h, sign),
                )
                copy.start()
                sends.append(copy)
                arriving[h, d, p, step] = copy
        for h, d, p in CHAINS:
            if step <= chain_length(d, p) + 1 and (step > 1 or d == 0):
                visit(h, wrap(ring[h] - (1 - 2 * d) * (step - 1)), p)
        if step <= N // 2:
            yield


def gather_sems(*lead):
    shapes = [(2, N - 1)] * 2 + [CHAIN_SEMS] * 2
    return [pltpu.SemaphoreType.DMA(lead + shape) for shape in shapes]


def exchange(sources, targets, sends, send_sem, recv_sem, devices):
    copies = []
    for i, device in enumerate(devices):
        copy = remote(sources(i), targets(i), send_sem.at[i], recv_sem.at[i], device)
        copy.start()
        copies.append(copy)
    sends += copies
    return copies


def front_kernel(
    factor_ref, wide_ref, left_ref, gram_ref,
    got, partial_ref, landed, local, first, second, mine, slice_ref, *sems,
):
    y, z, tp = place()
    gather_sem, (s1, r1, s2, r2), gram_sem, spread_sem = (
        sems[:4], sems[4:8], sems[8:14], sems[14:],
    )
    greet(all_peers())
    sends = []

    partial_ref[...] = jnp.zeros_like(partial_ref)

    def add_terms(h, index, part):
        part = pl.ds(part * WIDTH, WIDTH)
        block = wide_ref[h, index, part].reshape(WIDTH * HALF, wide_ref.shape[-1])
        rows = got[h, index, part].reshape(WIDTH * HALF, RANK)
        partial_ref[...] += lax.dot_general(
            block, rows, (((0,), (0,)), ((), ())), preferred_element_type=jnp.float32
        )

    for _ in gather_plane(factor_ref, got, gather_sem, add_terms, sends):
        pass

    def rows(index):
        return pl.ds(pl.multiple_of(index * HALF, HALF), HALF)

    others = [tp_device(k) for k in range(1, N)]
    copies = exchange(
        lambda i: partial_ref.at[rows(wrap(tp + i + 1))], lambda i: landed.at[i], sends, s1, r1, others
    )
    total = partial_ref[rows(tp), :]
    for i, copy in enumerate(copies):
        copy.wait_recv()
        total = total + landed[i]
    left_ref[rows(tp), :] = total
    copies = exchange(
        lambda i: left_ref.at[rows(tp)], lambda i: left_ref.at[rows(tp)], sends, s2, r2, others
    )
    for copy in copies:
        copy.wait_recv()

    size = RANK // N
    at = pl.ds(pl.multiple_of(tp // 2 * BLOCK, BLOCK), BLOCK)
    left = left_ref[...]
    local[...] = full_dot(left_ref[:, at], left, ((0,), (0,)))
    half = RANK // 2
    start = lax.rem(tp, 2) * size
    ring, across = (y, z), (z, y)

    def piece(index, base=0):
        return pl.ds(pl.multiple_of(base + index * N, N), N)

    def lanes(h):
        return pl.ds(h * half, half)

    groups = [[line_device(1 - h, k) for k in range(1, N)] for h in range(2)]
    turned = [[line_device(h, k) for k in range(1, N)] for h in range(2)]
    copies = [
        exchange(
            lambda i, h=h: local.at[piece(wrap(across[h] + i + 1), start), lanes(h)],
            lambda i, h=h: first.at[h, i], sends, gram_sem[0].at[h], gram_sem[1].at[h], groups[h],
        )
        for h in range(2)
    ]
    for h in range(2):
        total = local[piece(across[h], start), h * half : (h + 1) * half]
        for i, copy in enumerate(copies[h]):
            copy.wait_recv()
            total = total + first[h, i]
        mine[h] = total
        second[h, ring[h]] = total
        copies[h] = exchange(
            lambda i, h=h: mine.at[h], lambda i, h=h: second.at[h, ring[h]],
            sends, gram_sem[2].at[h], gram_sem[3].at[h], turned[h],
        )
    for h in range(2):
        for copy in copies[h]:
            copy.wait_recv()
        total = second[h, 0]
        for k in range(1, N):
            total = total + second[h, k]
        slice_ref[piece(across[h]), h * half : (h + 1) * half] = total
        ref = slice_ref.at[piece(across[h]), lanes(h)]
        copies[h] = exchange(
            lambda i: ref, lambda i: ref, sends, gram_sem[4].at[h], gram_sem[5].at[h], groups[h]
        )
    for h in range(2):
        for copy in copies[h]:
            copy.wait_recv()

    sibling = (lax.axis_index("fsdp"), tp + 1 - 2 * lax.rem(tp, 2))

    def slab(index):
        return gram_ref.at[pl.ds(pl.multiple_of(index * size, size), size)]

    far = exchange(
        lambda i: slice_ref, lambda i: slab(tp), sends, spread_sem[0], spread_sem[1],
        [tp_device(2 * k) for k in range(1, N // 2)],
    )
    near = [remote(slice_ref, slab(tp), spread_sem[2].at[0], spread_sem[3].at[0], sibling)]
    near[0].start()
    gram_ref[pl.ds(pl.multiple_of(tp * size, size), size), :] = slice_ref[...]
    for k in (1, 3, 2):
        far[k - 1].wait_recv()
        ref = slab(wrap(tp - 2 * k))
        copy = remote(ref, ref, spread_sem[2].at[k], spread_sem[3].at[k], sibling)
        copy.start()
        near.append(copy)
    for copy in near:
        copy.wait_recv()
    for copy in sends + near:
        copy.wait_send()


def front(factor, wide):
    rows = wide.shape[-1]
    f32 = jnp.float32
    return pl.pallas_call(
        front_kernel,
        out_shape=(
            jax.ShapeDtypeStruct((rows, RANK), f32),
            jax.ShapeDtypeStruct((RANK, RANK), f32),
        ),
        in_specs=[VMEM, VMEM],
        out_specs=(VMEM, VMEM),
        scratch_shapes=[
            pltpu.VMEM((2, N, N, HALF, RANK), jnp.bfloat16),
            pltpu.VMEM((rows, RANK), f32),
            pltpu.VMEM((N - 1, HALF, RANK), f32),
            pltpu.VMEM((BLOCK, RANK), f32),
            pltpu.VMEM((2, N - 1, N, RANK // 2), f32),
            pltpu.VMEM((2, N, N, RANK // 2), f32),
            pltpu.VMEM((2, N, RANK // 2), f32),
            pltpu.VMEM((RANK // N, RANK), f32),
        ]
        + gather_sems()
        + [pltpu.SemaphoreType.DMA((N - 1,)) for _ in range(4)]
        + [pltpu.SemaphoreType.DMA((2, N - 1)) for _ in range(6)]
        + [pltpu.SemaphoreType.DMA((N // 2,)) for _ in range(4)],
        compiler_params=params(0),
        name="front",
    )(factor, wide)


BLOCK = 128
BASE = 8
PAUSES = (4, 10)
BLOCKS = RANK // BLOCK


def small_inverse(panel, first):
    wide = (BASE, BLOCK)
    entry = {
        (i, j): jnp.broadcast_to(panel[i : i + 1, first + j : first + j + 1], wide)
        for i in range(BASE)
        for j in range(i + 1)
    }
    lower, inverse, scale = {}, {}, {}
    for j in range(BASE):
        pivot = entry[j, j]
        guess = lax.rsqrt(pivot)
        scale[j] = guess * (1.5 - 0.5 * ((pivot * guess) * guess))
        for i in range(j + 1, BASE):
            lower[i, j] = entry[i, j] * scale[j]
        for i in range(j + 1, BASE):
            for m in range(j + 1, i + 1):
                entry[i, m] = entry[i, m] - lower[i, j] * lower[m, j]
    for j in range(BASE):
        inverse[j, j] = scale[j]
        for i in range(j + 1, BASE):
            total = lower[i, j] * inverse[j, j]
            for m in range(j + 1, i):
                total = total + lower[i, m] * inverse[m, j]
            inverse[i, j] = -(scale[i] * total)
    index = lax.broadcasted_iota(jnp.int32, wide, 0)
    columns, rows = [], []
    for j in range(BASE):
        column = jnp.zeros(wide, jnp.float32)
        row = jnp.zeros(wide, jnp.float32)
        for i in range(j, BASE):
            column = jnp.where(index == i, inverse[i, j], column)
        for i in range(j + 1):
            row = jnp.where(index == i, inverse[j, i], row)
        columns.append(column)
        rows.append(row)
    return columns, rows


def add_up(terms):
    while len(terms) > 1:
        terms = [sum(terms[i + 1 : i + 2], terms[i]) for i in range(0, len(terms), 2)]
    return terms[0]


def combine(factors, panel):
    return [
        add_up([factors[m] * piece[m : m + 1, :] for m in range(BASE)]) for piece in panel
    ]


def block_inverse(block):
    row = lax.broadcasted_iota(jnp.int32, (BLOCK, BLOCK), 0)
    column = lax.broadcasted_iota(jnp.int32, (BLOCK, BLOCK), 1)
    unit = jnp.where(row == column, 1.0, 0.0).astype(jnp.float32)
    count = BLOCK // BASE
    panels = [
        [matrix[b * BASE : (b + 1) * BASE, :] for matrix in (block, unit)] for b in range(count)
    ]
    solved = []
    for b in range(count):
        first = b * BASE
        columns, rows = small_inverse(panels[b][0], first)
        done = combine(columns, panels[b])
        solved.append(done[1])
        if b + 1 == count:
            break
        again = combine(rows, done)
        ahead = panels[b + 1]
        factors = [
            jnp.broadcast_to(ahead[0][:, first + m : first + m + 1], (BASE, BLOCK))
            for m in range(BASE)
        ]
        panels[b + 1] = [old - new for old, new in zip(ahead, combine(factors, again))]
        if b in PAUSES:
            yield
        if b + 2 == count:
            continue
        multiplier = jnp.concatenate([panels[c][0] for c in range(b + 2, count)], axis=0)
        parts = [jnp.concatenate(again, axis=1)]
        parts.append(jnp.zeros((BLOCK - first - BASE, 2 * BLOCK), jnp.float32))
        if first:
            parts.insert(0, jnp.zeros((first, 2 * BLOCK), jnp.float32))
        change = jnp.dot(
            multiplier, jnp.concatenate(parts, axis=0), precision=HIGHEST,
            preferred_element_type=jnp.float32,
        )
        for c in range(b + 2, count):
            at = (c - b - 2) * BASE
            panels[c] = [
                old - change[at : at + BASE, i * BLOCK : (i + 1) * BLOCK]
                for i, old in enumerate(panels[c])
            ]
    return jnp.where(row >= column, jnp.concatenate(solved, axis=0), 0.0)


def full_dot(x, y, dims):
    return lax.dot_general(
        x, y, (dims, ((), ())), precision=HIGHEST, preferred_element_type=jnp.float32
    )


def right_block(c, wide_ref, ortho_ref, mine_ref, right_ref, squares_ref, refs, sems, sends):
    chain, summed, landed = (ref.at[c] for ref in refs)
    send1, recv1, send2, recv2 = (sem.at[c] for sem in sems[:4])
    y, z, _ = place()
    ring, across = (y, z), (z, y)
    columns = slice(c * BLOCK, (c + 1) * BLOCK)

    def own(h, target, part):
        block = wide_ref[h, wrap(target), pl.ds(part * WIDTH, WIDTH)]
        product = jnp.dot(
            block.reshape(WIDTH * HALF, block.shape[-1]), ortho_ref[:, columns],
            preferred_element_type=jnp.float32,
        )
        return product.reshape(WIDTH, HALF, BLOCK)

    arriving = {}

    def pass_on(h, d, p, step):
        copy = remote(
            chain.at[h, d, step - 1, p], chain.at[h, d, step, p],
            send1.at[h, d, step - 1, p], recv1.at[h, d, step - 1, p], line_device(h, 1 - 2 * d),
        )
        copy.start()
        sends.append(copy)
        arriving[h, d, p, step] = copy

    for h, d, p in CHAINS:
        term = own(h, ring[h] + (1 - 2 * d) * chain_length(d, p), p)
        chain[h, d, 0, p] = term.astype(jnp.bfloat16)
        pass_on(h, d, p, 1)
    yield
    for step in range(1, N // 2):
        for h, d, p in CHAINS:
            length = chain_length(d, p)
            if step < length:
                term = own(h, ring[h] + (1 - 2 * d) * (length - step), p)
                arriving[h, d, p, step].wait_recv()
                term = term + chain[h, d, step, p].astype(jnp.float32)
                chain[h, d, step, p] = term.astype(jnp.bfloat16)
                pass_on(h, d, p, step + 1)
        yield
    for h in range(2):
        for p in range(PARTS):
            term = own(h, ring[h], p)
            for d in range(2):
                length = chain_length(d, p)
                arriving[h, d, p, length].wait_recv()
                term = term + chain[h, d, length, p].astype(jnp.float32)
            summed[h, p * WIDTH : (p + 1) * WIDTH] = term.astype(jnp.bfloat16)
    second = [
        exchange(
            lambda i, h=h: summed.at[h, wrap(across[h] + i + 1)], lambda i, h=h: landed.at[h, i],
            sends, send2.at[h], recv2.at[h], [line_device(1 - h, k) for k in range(1, N)],
        )
        for h in range(2)
    ]
    yield
    for h in range(2):
        total = summed[h, across[h]].astype(jnp.float32)
        for i, copy in enumerate(second[h]):
            copy.wait_recv()
            total = total + landed[h, i].astype(jnp.float32)
        mine_ref[c, h] = total.astype(jnp.bfloat16)

    def add_squares(h, index, part):
        block = right_ref[c, h, index, pl.ds(part * WIDTH, WIDTH)].astype(jnp.float32)
        block = block.reshape(WIDTH * HALF // N, N, BLOCK)
        squares_ref[:, columns] += jnp.sum(block * block, axis=0)

    yield from gather_plane(
        mine_ref.at[c], right_ref.at[c], [sem.at[c] for sem in sems[4:]], add_squares, sends
    )


def right_kernel(
    gram_ref, left_ref, wide_ref, ortho_ref, mine_ref, right_ref, squares_ref,
    rest, tail, chain, summed, landed, squares, spread, send, recv, *sems,
):
    greet(all_peers())
    sends, active = [], []

    def advance():
        for work in list(active):
            if next(work, active) is active:
                active.remove(work)

    rest[...] = gram_ref[...]
    tail[...] = left_ref[...]
    squares[...] = jnp.zeros_like(squares)
    for c in range(BLOCKS):
        at, end = c * BLOCK, (c + 1) * BLOCK
        elimination = block_inverse(rest[at:end, at:end])
        while True:
            try:
                next(elimination)
            except StopIteration as result:
                inverse = result.value
                break
            advance()
        done = full_dot(tail[:, at:end], inverse, ((1,), (1,)))
        ortho_ref[:, at:end] = done.astype(ortho_ref.dtype)
        advance()
        work = right_block(
            c, wide_ref, ortho_ref, mine_ref, right_ref, squares, (chain, summed, landed), sems, sends
        )
        next(work)
        active.append(work)
        if end == RANK:
            break
        panel = full_dot(inverse, rest[at:end, end:], ((1,), (0,)))
        for start in range(end, RANK, BLOCK):
            piece = panel[:, start - end : start - end + BLOCK]
            rest[start : start + BLOCK, start:] -= full_dot(
                piece, panel[:, start - end :], ((0,), (0,))
            )
        tail[:, end:] -= full_dot(done, panel, ((1,), (0,)))
    while active:
        advance()

    tp = lax.axis_index("tp")
    copies = exchange(
        lambda i: squares, lambda i: spread.at[tp], sends, send, recv,
        [tp_device(k) for k in range(1, N)],
    )
    spread[tp] = squares[...]
    for copy in copies:
        copy.wait_recv()
    total = spread[0]
    for k in range(1, N):
        total = total + spread[k]
    squares_ref[...] = total
    for copy in sends:
        copy.wait_send()


def make_right(gram, left, wide):
    rows = left.shape[0]
    f32, bf16 = jnp.float32, jnp.bfloat16
    return pl.pallas_call(
        right_kernel,
        out_shape=(
            jax.ShapeDtypeStruct((rows, RANK), bf16),
            jax.ShapeDtypeStruct((BLOCKS, 2, HALF, BLOCK), bf16),
            jax.ShapeDtypeStruct((BLOCKS, 2, N, N, HALF, BLOCK), bf16),
            jax.ShapeDtypeStruct((N, RANK), f32),
        ),
        in_specs=[VMEM] * 3,
        out_specs=(VMEM,) * 4,
        scratch_shapes=[
            pltpu.VMEM((RANK, RANK), f32),
            pltpu.VMEM((rows, RANK), f32),
            pltpu.VMEM((BLOCKS, 2, 2, N // 2 + 1, PARTS, WIDTH, HALF, BLOCK), bf16),
            pltpu.VMEM((BLOCKS, 2, N, HALF, BLOCK), bf16),
            pltpu.VMEM((BLOCKS, 2, N - 1, HALF, BLOCK), bf16),
            pltpu.VMEM((N, RANK), f32),
            pltpu.VMEM((N, N, RANK), f32),
            pltpu.SemaphoreType.DMA((N - 1,)),
            pltpu.SemaphoreType.DMA((N - 1,)),
            pltpu.SemaphoreType.DMA((BLOCKS,) + CHAIN_SEMS),
            pltpu.SemaphoreType.DMA((BLOCKS,) + CHAIN_SEMS),
            pltpu.SemaphoreType.DMA((BLOCKS, 2, N - 1)),
            pltpu.SemaphoreType.DMA((BLOCKS, 2, N - 1)),
        ]
        + gather_sems(BLOCKS),
        compiler_params=params(1),
        name="make_right",
    )(gram, left, wide)


def finish_kernel(
    squares_ref, first_ref, second_ref, mine_ref, ortho_ref, gradient_ref, momentum_ref,
    update_ref, new_ref, factor_ref, factor,
):
    squares = jnp.sum(squares_ref[...], axis=0, keepdims=True)
    norms = jnp.sqrt(squares + 1e-06)
    gain = math.sqrt(FFW) / norms
    ortho = ortho_ref[...]
    scaled = (ortho.astype(jnp.float32) * (norms / math.sqrt(FFW))).astype(jnp.bfloat16)
    stacked = jnp.concatenate([ortho, scaled], axis=0)
    group = 4
    for c in range(BLOCKS):
        columns = slice(c * BLOCK, (c + 1) * BLOCK)

        def joined(top, bottom):
            top = top.astype(jnp.float32) * gain[:, columns]
            bottom = bottom.astype(jnp.float32) * gain[:, columns]
            return [top, bottom[: ROWS - HALF]]

        factor_ref[:, columns] = jnp.concatenate(
            joined(mine_ref[c, 0], mine_ref[c, 1]), axis=0
        ).astype(jnp.bfloat16)
        for y in range(first_ref.shape[2]):
            for z in range(0, N, group):
                pieces = []
                for i in range(z, z + group):
                    pieces += joined(first_ref[c, 0, y, i], second_ref[c, 0, i, y])
                start = (y * N + z) * ROWS
                factor[start : start + group * ROWS, columns] = jnp.concatenate(
                    pieces, axis=0
                ).astype(jnp.bfloat16)
    combined = lax.dot_general(
        stacked, factor[...], (((1,), (1,)), ((), ())), preferred_element_type=jnp.float32
    )
    rows = ortho.shape[0]
    update_ref[...] = (math.sqrt(D / RANK) * combined[:rows]).astype(jnp.bfloat16)
    whole = momentum_ref[...] + gradient_ref[...].astype(jnp.float32)
    new_ref[...] = whole - 0.05 * combined[rows:]


def finish(squares, right, mine, ortho, gradient, momentum):
    steps = 2
    rows, columns = gradient.shape
    some = N // steps
    whole = lambda *shape: pl.BlockSpec(shape, lambda i: (0,) * len(shape))
    tile = pl.BlockSpec((rows, columns // steps), lambda i: (0, i))
    return pl.pallas_call(
        finish_kernel,
        grid=(steps,),
        out_shape=(
            jax.ShapeDtypeStruct((rows, columns), jnp.bfloat16),
            jax.ShapeDtypeStruct((rows, columns), jnp.float32),
            jax.ShapeDtypeStruct((ROWS, RANK), jnp.bfloat16),
        ),
        in_specs=[
            whole(N, RANK),
            pl.BlockSpec((BLOCKS, 1, some, N, HALF, BLOCK), lambda i: (0, 0, i, 0, 0, 0)),
            pl.BlockSpec((BLOCKS, 1, N, some, HALF, BLOCK), lambda i: (0, 1, 0, i, 0, 0)),
            whole(BLOCKS, 2, HALF, BLOCK),
            whole(rows, RANK),
            tile,
            tile,
        ],
        out_specs=(tile, tile, whole(ROWS, RANK)),
        scratch_shapes=[pltpu.VMEM((columns // steps, RANK), jnp.bfloat16)],
        compiler_params=pltpu.CompilerParams(vmem_limit_bytes=48 * 2**20),
        name="finish",
    )(squares, right, right, mine, ortho, gradient, momentum)


def body(gradient, momentum, right_factor):
    wide = (momentum + gradient.astype(jnp.float32)).astype(jnp.bfloat16)
    row_count = wide.shape[0]
    blocks = wide.T.reshape(N, N, ROWS, row_count)
    blocks = jnp.pad(blocks, ((0, 0), (0, 0), (0, PAD - ROWS), (0, 0)))
    blocks = jnp.stack([blocks[:, :, :HALF], jnp.swapaxes(blocks[:, :, HALF:], 0, 1)])
    factor = jnp.pad(right_factor, ((0, PAD - ROWS), (0, 0))).reshape(2, HALF, RANK)
    left, gram = front(factor, blocks)
    ortho, mine, right, squares = make_right(gram, left, blocks)
    return finish(squares, right, mine, ortho, gradient, momentum)


def solution(mesh):
    return jax.shard_map(
        body,
        mesh=mesh,
        in_specs=(P("fsdp", "tp"), P("fsdp", "tp"), P(("tp", "fsdp"), None)),
        out_specs=(P("fsdp", "tp"), P("fsdp", "tp"), P(("tp", "fsdp"), None)),
        check_vma=False,
    )
```

```python
import functools
import math

import jax
import jax.numpy as jnp
from jax import lax
from jax.experimental import pallas as pl
from jax.experimental.pallas import tpu as pltpu
from jax.sharding import PartitionSpec as P

D = 8192
FFW = 14336
RANK = 512
N = 8
ROWS = 28
PAD = 32
HALF = 16
MESH = pl.DeviceIdType.MESH
HIGHEST = lax.Precision.HIGHEST
VMEM = pl.BlockSpec(memory_space=pltpu.VMEM)


def params(collective_id):
    return pltpu.CompilerParams(
        collective_id=collective_id, has_side_effects=True, vmem_limit_bytes=48 * 2**20
    )


def wrap(index):
    return lax.rem(index + 2 * N, N)


def greet_start(peers):
    barrier = pltpu.get_barrier_semaphore()
    for peer in peers:
        pl.semaphore_signal(barrier, inc=1, device_id=peer, device_id_type=MESH)


def greet_end(peers):
    pl.semaphore_wait(pltpu.get_barrier_semaphore(), len(peers))


def remote(src, dst, send_sem, recv_sem, device):
    return pltpu.make_async_remote_copy(
        src_ref=src, dst_ref=dst, send_sem=send_sem, recv_sem=recv_sem,
        device_id=device, device_id_type=MESH,
    )


def place():
    fsdp = lax.axis_index("fsdp")
    return fsdp // N, lax.rem(fsdp, N), lax.axis_index("tp")


def line_device(axis, offset):
    y, z, tp = place()
    if axis == 0:
        return (wrap(y + offset) * N + z, tp)
    return (y * N + wrap(z + offset), tp)


def tp_device(offset):
    return (lax.axis_index("fsdp"), wrap(lax.axis_index("tp") + offset))


def all_peers():
    plane = [line_device(axis, k) for axis in range(2) for k in range(1, N)]
    return plane + [tp_device(k) for k in range(1, N)]


HALVES = (pl.ds(0, N // 2), pl.ds(N // 2, N // 2))
CHAINS = [(h, d) for h in range(2) for d in range(2)]


def signs(direction):
    return 1 - 2 * direction


def arrived(ref, sem, spare, device):
    remote(ref, ref, spare, sem, device).wait_recv()


def left_here(ref, sem, spare, device):
    remote(ref, ref, sem, spare, device).wait_send()


def exchange(source, target, send_sem, recv_sem, devices):
    for i, device in enumerate(devices):
        remote(source(i), target(i), send_sem, recv_sem, device).start()


def gather_plane(mine, out, sends, direct, landing, visit):
    y, z, _ = place()
    ring, across = (y, z), (z, y)
    for k in range(1, N):
        for h in range(2):
            remote(
                mine.at[h], out.at[h, ring[h], across[h]], sends.at[0], direct.at[h],
                line_device(1 - h, k),
            ).start()
    for h in range(2):
        out[h, ring[h], across[h]] = mine[h]
    for h in range(2):
        arrived(
            out.at[h, ring[h], pl.ds(0, N - 1)], direct.at[h], sends.at[0], line_device(1 - h, 1)
        )
    arriving = {}
    for step in range(1, N // 2 + 1):
        for h, d in CHAINS:
            if step > 1:
                arriving[h, d].wait_recv()
            index = wrap(ring[h] - signs(d) * (step - 1))
            ref = out.at[h, index] if step < N // 2 else out.at[h, index, HALVES[d]]
            arriving[h, d] = remote(
                ref, ref, sends.at[1], landing.at[h, d, step - 1], line_device(h, signs(d))
            )
            arriving[h, d].start()
        for h, d in CHAINS:
            if step > 1 or d == 0:
                visit(h, wrap(ring[h] - signs(d) * (step - 1)))
    for h, d in CHAINS:
        arriving[h, d].wait_recv()
        if d == 1:
            visit(h, wrap(ring[h] + N // 2))
    device = line_device(0, 1)
    left_here(out.at[:, 0, pl.ds(0, N - 1)], sends.at[0], direct.at[0], device)
    left_here(out.at[:, pl.ds(0, N - 1)], sends.at[1], direct.at[0], device)


def gather_sems():
    return [
        pltpu.SemaphoreType.DMA((2,)),
        pltpu.SemaphoreType.DMA((2,)),
        pltpu.SemaphoreType.DMA((2, 2, N // 2)),
    ]


def front_kernel(
    factor_ref, wide_ref, left_ref, gram_ref,
    got, partial_ref, landed, local, first, second, mine, slice_ref,
    gather_sends, direct, landing, sends, recvs,
):
    y, z, tp = place()
    greet_start(all_peers())
    partial_ref[...] = jnp.zeros_like(partial_ref)
    greet_end(all_peers())

    def add_terms(h, index):
        block = wide_ref[h, index].reshape(N * HALF, wide_ref.shape[-1])
        rows = got[h, index].reshape(N * HALF, RANK)
        partial_ref[...] += lax.dot_general(
            block, rows, (((0,), (0,)), ((), ())), preferred_element_type=jnp.float32
        )

    gather_plane(factor_ref, got, gather_sends, direct, landing, add_terms)

    def rows(index):
        return pl.ds(pl.multiple_of(index * HALF, HALF), HALF)

    others = [tp_device(k) for k in range(1, N)]
    exchange(
        lambda i: partial_ref.at[rows(wrap(tp + i + 1))], lambda i: landed.at[i],
        sends.at[0], recvs.at[0], others,
    )
    arrived(landed, recvs.at[0], sends.at[0], others[0])
    total = partial_ref[rows(tp), :]
    for i in range(N - 1):
        total = total + landed[i]
    left_ref[rows(tp), :] = total
    exchange(
        lambda i: left_ref.at[rows(tp)], lambda i: left_ref.at[rows(tp)],
        sends.at[1], recvs.at[1], others,
    )
    most = left_ref.at[pl.ds(0, (N - 1) * HALF)]
    arrived(most, recvs.at[1], sends.at[1], others[0])

    size = RANK // N
    at = pl.ds(pl.multiple_of(tp // 2 * BLOCK, BLOCK), BLOCK)
    local[...] = full_dot(left_ref[:, at], left_ref[...], ((0,), (0,)))
    start = lax.rem(tp, 2) * size

    def piece(index, base=0):
        return pl.ds(pl.multiple_of(base + index * N, N), N)

    along = [[line_device(axis, k) for k in range(1, N)] for axis in range(2)]
    exchange(
        lambda i: local.at[piece(wrap(z + i + 1), start)], lambda i: first.at[i],
        sends.at[2], recvs.at[2], along[1],
    )
    arrived(first, recvs.at[2], sends.at[2], along[1][0])
    total = local[piece(z, start), :]
    for i in range(N - 1):
        total = total + first[i]
    mine[...] = total
    second[y] = total
    exchange(
        lambda i: mine, lambda i: second.at[y], sends.at[3], recvs.at[3], along[0]
    )
    arrived(second.at[pl.ds(0, N - 1)], recvs.at[3], sends.at[3], along[0][0])
    total = second[0]
    for k in range(1, N):
        total = total + second[k]
    slice_ref[piece(z), :] = total
    ref = slice_ref.at[piece(z)]
    exchange(lambda i: ref, lambda i: ref, sends.at[4], recvs.at[4], along[1])
    some = slice_ref.at[pl.ds(0, (N - 1) * N)]
    arrived(some, recvs.at[4], sends.at[4], along[1][0])

    sibling = (lax.axis_index("fsdp"), tp + 1 - 2 * lax.rem(tp, 2))

    def slab(index, begin=0, count=size):
        begin = pl.multiple_of(wrap(index) * size + begin, size // 2)
        return gram_ref.at[pl.ds(begin, count)]

    far = []
    for d in range(2):
        far.append(
            remote(slice_ref, slab(tp), sends.at[5], recvs.at[5 + d], tp_device(2 * signs(d)))
        )
        far[d].start()
    remote(slice_ref, slab(tp), sends.at[5], recvs.at[9], sibling).start()
    gram_ref[pl.ds(pl.multiple_of(tp * size, size), size), :] = slice_ref[...]
    half = []
    for d in range(2):
        far[d].wait_recv()
        ref = slab(tp - 2 * signs(d), d * (size // 2), size // 2)
        half.append(remote(ref, ref, sends.at[5], recvs.at[7 + d], tp_device(2 * signs(d))))
        half[d].start()
        ref = slab(tp - 2 * signs(d))
        remote(ref, ref, sends.at[5], recvs.at[9], sibling).start()
    for d in range(2):
        half[d].wait_recv()
    ref = slab(tp + N // 2)
    remote(ref, ref, sends.at[5], recvs.at[9], sibling).start()
    arrived(gram_ref.at[pl.ds(0, N // 2 * size)], recvs.at[9], sends.at[5], sibling)

    left_here(landed, sends.at[0], recvs.at[0], sibling)
    left_here(most, sends.at[1], recvs.at[0], sibling)
    left_here(first, sends.at[2], recvs.at[0], sibling)
    left_here(second.at[pl.ds(0, N - 1)], sends.at[3], recvs.at[0], sibling)
    left_here(some, sends.at[4], recvs.at[0], sibling)
    left_here(gram_ref.at[pl.ds(0, (N - 1) * size)], sends.at[5], recvs.at[0], sibling)


def front(factor, wide):
    rows = wide.shape[-1]
    f32 = jnp.float32
    return pl.pallas_call(
        front_kernel,
        out_shape=(
            jax.ShapeDtypeStruct((rows, RANK), f32),
            jax.ShapeDtypeStruct((RANK, RANK), f32),
        ),
        in_specs=[VMEM, VMEM],
        out_specs=(VMEM, VMEM),
        scratch_shapes=[
            pltpu.VMEM((2, N, N, HALF, RANK), jnp.bfloat16),
            pltpu.VMEM((rows, RANK), f32),
            pltpu.VMEM((N - 1, HALF, RANK), f32),
            pltpu.VMEM((BLOCK, RANK), f32),
            pltpu.VMEM((N - 1, N, RANK), f32),
            pltpu.VMEM((N, N, RANK), f32),
            pltpu.VMEM((N, RANK), f32),
            pltpu.VMEM((RANK // N, RANK), f32),
        ]
        + gather_sems()
        + [pltpu.SemaphoreType.DMA((6,)), pltpu.SemaphoreType.DMA((10,))],
        compiler_params=params(0),
        name="front",
    )(factor, wide)


BLOCK = 128
BASE = 8


def small_inverse(panel, first):
    wide = (BASE, BLOCK)
    entry = {
        (i, j): jnp.broadcast_to(panel[i : i + 1, first + j : first + j + 1], wide)
        for i in range(BASE)
        for j in range(i + 1)
    }
    lower, inverse, scale = {}, {}, {}
    for j in range(BASE):
        pivot = entry[j, j]
        guess = lax.rsqrt(pivot)
        scale[j] = guess * (1.5 - 0.5 * ((pivot * guess) * guess))
        for i in range(j + 1, BASE):
            lower[i, j] = entry[i, j] * scale[j]
        for i in range(j + 1, BASE):
            for m in range(j + 1, i + 1):
                entry[i, m] = entry[i, m] - lower[i, j] * lower[m, j]
    for j in range(BASE):
        inverse[j, j] = scale[j]
        for i in range(j + 1, BASE):
            total = lower[i, j] * inverse[j, j]
            for m in range(j + 1, i):
                total = total + lower[i, m] * inverse[m, j]
            inverse[i, j] = -(scale[i] * total)
    index = lax.broadcasted_iota(jnp.int32, wide, 0)
    columns, rows = [], []
    for j in range(BASE):
        column = jnp.zeros(wide, jnp.float32)
        row = jnp.zeros(wide, jnp.float32)
        for i in range(j, BASE):
            column = jnp.where(index == i, inverse[i, j], column)
        for i in range(j + 1):
            row = jnp.where(index == i, inverse[j, i], row)
        columns.append(column)
        rows.append(row)
    return columns, rows


def add_up(terms):
    while len(terms) > 1:
        terms = [sum(terms[i + 1 : i + 2], terms[i]) for i in range(0, len(terms), 2)]
    return terms[0]


def combine(factors, panel):
    return [
        add_up([factors[m] * piece[m : m + 1, :] for m in range(BASE)]) for piece in panel
    ]


def block_inverse(block):
    row = lax.broadcasted_iota(jnp.int32, (BLOCK, BLOCK), 0)
    column = lax.broadcasted_iota(jnp.int32, (BLOCK, BLOCK), 1)
    unit = jnp.where(row == column, 1.0, 0.0).astype(jnp.float32)
    count = BLOCK // BASE
    panels = [
        [matrix[b * BASE : (b + 1) * BASE, :] for matrix in (block, unit)] for b in range(count)
    ]
    solved = []
    for b in range(count):
        first = b * BASE
        columns, rows = small_inverse(panels[b][0], first)
        done = combine(columns, panels[b])
        solved.append(done[1])
        if b + 1 == count:
            break
        again = combine(rows, done)
        ahead = panels[b + 1]
        factors = [
            jnp.broadcast_to(ahead[0][:, first + m : first + m + 1], (BASE, BLOCK))
            for m in range(BASE)
        ]
        panels[b + 1] = [old - new for old, new in zip(ahead, combine(factors, again))]
        if b + 2 == count:
            continue
        multiplier = jnp.concatenate([panels[c][0] for c in range(b + 2, count)], axis=0)
        parts = [jnp.concatenate(again, axis=1)]
        parts.append(jnp.zeros((BLOCK - first - BASE, 2 * BLOCK), jnp.float32))
        if first:
            parts.insert(0, jnp.zeros((first, 2 * BLOCK), jnp.float32))
        change = jnp.dot(
            multiplier, jnp.concatenate(parts, axis=0), precision=HIGHEST,
            preferred_element_type=jnp.float32,
        )
        for c in range(b + 2, count):
            at = (c - b - 2) * BASE
            panels[c] = [
                old - change[at : at + BASE, i * BLOCK : (i + 1) * BLOCK]
                for i, old in enumerate(panels[c])
            ]
    return jnp.where(row >= column, jnp.concatenate(solved, axis=0), 0.0)


def full_dot(x, y, dims):
    return lax.dot_general(
        x, y, (dims, ((), ())), precision=HIGHEST, preferred_element_type=jnp.float32
    )


def ortho_kernel(gram_ref, left_ref, out_ref, rest, tail):
    rest[...] = gram_ref[...]
    tail[...] = left_ref[...]
    for at in range(0, RANK, BLOCK):
        end = at + BLOCK
        inverse = block_inverse(rest[at:end, at:end])
        done = full_dot(tail[:, at:end], inverse, ((1,), (1,)))
        out_ref[:, at:end] = done.astype(out_ref.dtype)
        if end == RANK:
            break
        panel = full_dot(inverse, rest[at:end, end:], ((1,), (0,)))
        for start in range(end, RANK, BLOCK):
            piece = panel[:, start - end : start - end + BLOCK]
            rest[start : start + BLOCK, start:] -= full_dot(
                piece, panel[:, start - end :], ((0,), (0,))
            )
        tail[:, end:] -= full_dot(done, panel, ((1,), (0,)))


def orthonormalize(gram, left):
    return pl.pallas_call(
        ortho_kernel,
        out_shape=jax.ShapeDtypeStruct(left.shape, jnp.bfloat16),
        in_specs=[VMEM, VMEM],
        out_specs=VMEM,
        scratch_shapes=[
            pltpu.VMEM((RANK, RANK), jnp.float32),
            pltpu.VMEM(left.shape, jnp.float32),
        ],
        compiler_params=pltpu.CompilerParams(vmem_limit_bytes=48 * 2**20),
        name="orthonormalize",
    )(gram, left)


LINKS = N // 2 + 1


def right_kernel(
    wide_ref, ortho_ref, mine_ref, right_ref, squares_ref,
    chain, terms, summed, landed, squares, spread,
    gather_sends, direct, landing, sends, chain_recv, recvs,
):
    y, z, tp = place()
    ring, across = (y, z), (z, y)
    greet_start(all_peers())

    def own(h, target):
        block = wide_ref[h, wrap(target)].reshape(N * HALF, wide_ref.shape[-1])
        product = jnp.dot(block, ortho_ref[...], preferred_element_type=jnp.float32)
        return product.reshape(N, HALF, RANK)

    arriving = {}

    def pass_on(h, d, step):
        at = LINKS * d + step
        source, target = chain.at[h, at - 1], chain.at[h, at]
        if step == 1:
            source, target = chain.at[h, at - 1, HALVES[d]], chain.at[h, at, HALVES[d]]
        arriving[h, d] = remote(
            source, target, sends.at[0], chain_recv.at[h, d, step - 1], line_device(h, signs(d))
        )
        arriving[h, d].start()

    middle = N // 2
    for h in range(2):
        term = own(h, ring[h] + middle).astype(jnp.bfloat16)
        chain[h, 0, :middle] = term[:middle]
        chain[h, LINKS, middle:] = term[middle:]
    squares[...] = jnp.zeros_like(squares)
    greet_end(all_peers())
    for h, d in CHAINS:
        pass_on(h, d, 1)
    for step in range(1, middle):
        for i, (h, d) in enumerate(CHAINS):
            terms[i] = own(h, ring[h] + signs(d) * (middle - step))
        for i, (h, d) in enumerate(CHAINS):
            at = LINKS * d + step
            arriving[h, d].wait_recv()
            if step == 1:
                here = slice(0, middle) if d == 0 else slice(middle, N)
                rest = slice(middle, N) if d == 0 else slice(0, middle)
                total = terms[i, here] + chain[h, at, here].astype(jnp.float32)
                chain[h, at, here] = total.astype(jnp.bfloat16)
                chain[h, at, rest] = terms[i, rest].astype(jnp.bfloat16)
            else:
                total = terms[i] + chain[h, at].astype(jnp.float32)
                chain[h, at] = total.astype(jnp.bfloat16)
            pass_on(h, d, step + 1)
    for h in range(2):
        terms[h] = own(h, ring[h])
    for h in range(2):
        for d in range(2):
            arriving[h, d].wait_recv()
        total = terms[h] + chain[h, middle].astype(jnp.float32)
        total = total + chain[h, LINKS + middle].astype(jnp.float32)
        summed[h] = total.astype(jnp.bfloat16)
        exchange(
            lambda i: summed.at[h, wrap(across[h] + i + 1)], lambda i: landed.at[h, i],
            sends.at[1], recvs.at[h], [line_device(1 - h, k) for k in range(1, N)],
        )
    device = line_device(0, 1)
    for h in range(2):
        arrived(landed.at[h], recvs.at[h], sends.at[1], device)
        total = summed[h, across[h]].astype(jnp.float32)
        for i in range(N - 1):
            total = total + landed[h, i].astype(jnp.float32)
        mine_ref[h] = total.astype(jnp.bfloat16)

    def add_squares(h, index):
        block = right_ref[h, index].astype(jnp.float32).reshape(N * HALF // N, N, RANK)
        squares[...] += jnp.sum(block * block, axis=0)

    gather_plane(mine_ref, right_ref, gather_sends, direct, landing, add_squares)

    exchange(
        lambda i: squares, lambda i: spread.at[tp], sends.at[2], recvs.at[2],
        [tp_device(k) for k in range(1, N)],
    )
    spread[tp] = squares[...]
    others = spread.at[pl.ds(0, N - 1)]
    arrived(others, recvs.at[2], sends.at[2], device)
    total = spread[0]
    for k in range(1, N):
        total = total + spread[k]
    squares_ref[...] = total
    left_here(chain.at[:, pl.ds(0, N - 1)], sends.at[0], recvs.at[0], device)
    left_here(landed, sends.at[1], recvs.at[0], device)
    left_here(others, sends.at[2], recvs.at[0], device)


def make_right(wide, ortho):
    f32, bf16 = jnp.float32, jnp.bfloat16
    return pl.pallas_call(
        right_kernel,
        out_shape=(
            jax.ShapeDtypeStruct((2, HALF, RANK), bf16),
            jax.ShapeDtypeStruct((2, N, N, HALF, RANK), bf16),
            jax.ShapeDtypeStruct((N, RANK), f32),
        ),
        in_specs=[VMEM] * 2,
        out_specs=(VMEM,) * 3,
        scratch_shapes=[
            pltpu.VMEM((2, 2 * LINKS, N, HALF, RANK), bf16),
            pltpu.VMEM((4, N, HALF, RANK), f32),
            pltpu.VMEM((2, N, HALF, RANK), bf16),
            pltpu.VMEM((2, N - 1, HALF, RANK), bf16),
            pltpu.VMEM((N, RANK), f32),
            pltpu.VMEM((N, N, RANK), f32),
        ]
        + gather_sems()
        + [
            pltpu.SemaphoreType.DMA((3,)),
            pltpu.SemaphoreType.DMA((2, 2, N // 2)),
            pltpu.SemaphoreType.DMA((3,)),
        ],
        compiler_params=params(1),
        name="make_right",
    )(wide, ortho)


def finish_kernel(
    squares_ref, first_ref, second_ref, mine_ref, ortho_ref, gradient_ref, momentum_ref,
    update_ref, new_ref, factor_ref, factor,
):
    squares = jnp.sum(squares_ref[...], axis=0, keepdims=True)
    norms = jnp.sqrt(squares + 1e-06)
    gain = math.sqrt(FFW) / norms
    ortho = ortho_ref[...]
    scaled = (ortho.astype(jnp.float32) * (norms / math.sqrt(FFW))).astype(jnp.bfloat16)
    stacked = jnp.concatenate([ortho, scaled], axis=0)
    group = 4

    def joined(top, bottom):
        top = top.astype(jnp.float32) * gain
        bottom = bottom.astype(jnp.float32) * gain
        return [top, bottom[: ROWS - HALF]]

    factor_ref[...] = jnp.concatenate(joined(mine_ref[0], mine_ref[1]), axis=0).astype(jnp.bfloat16)
    for y in range(first_ref.shape[1]):
        for z in range(0, N, group):
            pieces = []
            for i in range(z, z + group):
                pieces += joined(first_ref[0, y, i], second_ref[0, i, y])
            start = (y * N + z) * ROWS
            factor[start : start + group * ROWS, :] = jnp.concatenate(
                pieces, axis=0
            ).astype(jnp.bfloat16)
    combined = lax.dot_general(
        stacked, factor[...], (((1,), (1,)), ((), ())), preferred_element_type=jnp.float32
    )
    rows = ortho.shape[0]
    update_ref[...] = (math.sqrt(D / RANK) * combined[:rows]).astype(jnp.bfloat16)
    whole = momentum_ref[...] + gradient_ref[...].astype(jnp.float32)
    new_ref[...] = whole - 0.05 * combined[rows:]


def finish(squares, right, mine, ortho, gradient, momentum):
    steps = 2
    rows, columns = gradient.shape
    some = N // steps
    whole = lambda *shape: pl.BlockSpec(shape, lambda i: (0,) * len(shape))
    tile = pl.BlockSpec((rows, columns // steps), lambda i: (0, i))
    return pl.pallas_call(
        finish_kernel,
        grid=(steps,),
        out_shape=(
            jax.ShapeDtypeStruct((rows, columns), jnp.bfloat16),
            jax.ShapeDtypeStruct((rows, columns), jnp.float32),
            jax.ShapeDtypeStruct((ROWS, RANK), jnp.bfloat16),
        ),
        in_specs=[
            whole(N, RANK),
            pl.BlockSpec((1, some, N, HALF, RANK), lambda i: (0, i, 0, 0, 0)),
            pl.BlockSpec((1, N, some, HALF, RANK), lambda i: (1, 0, i, 0, 0)),
            whole(2, HALF, RANK),
            whole(rows, RANK),
            tile,
            tile,
        ],
        out_specs=(tile, tile, whole(ROWS, RANK)),
        scratch_shapes=[pltpu.VMEM((columns // steps, RANK), jnp.bfloat16)],
        compiler_params=pltpu.CompilerParams(vmem_limit_bytes=48 * 2**20),
        name="finish",
    )(squares, right, right, mine, ortho, gradient, momentum)


def body(gradient, momentum, right_factor):
    wide = (momentum + gradient.astype(jnp.float32)).astype(jnp.bfloat16)
    row_count = wide.shape[0]
    blocks = wide.T.reshape(N, N, ROWS, row_count)
    blocks = jnp.pad(blocks, ((0, 0), (0, 0), (0, PAD - ROWS), (0, 0)))
    blocks = jnp.stack([blocks[:, :, :HALF], jnp.swapaxes(blocks[:, :, HALF:], 0, 1)])
    factor = jnp.pad(right_factor, ((0, PAD - ROWS), (0, 0))).reshape(2, HALF, RANK)
    left, gram = front(factor, blocks)
    ortho = orthonormalize(gram, left)
    mine, right, squares = make_right(blocks, ortho)
    return finish(squares, right, mine, ortho, gradient, momentum)


def solution(mesh):
    return jax.shard_map(
        body,
        mesh=mesh,
        in_specs=(P("fsdp", "tp"), P("fsdp", "tp"), P(("tp", "fsdp"), None)),
        out_specs=(P("fsdp", "tp"), P("fsdp", "tp"), P(("tp", "fsdp"), None)),
        check_vma=False,
    )
```

```python
import functools
import math

import jax
import jax.numpy as jnp
from jax import lax
from jax.experimental import pallas as pl
from jax.experimental.pallas import tpu as pltpu
from jax.sharding import PartitionSpec as P

D = 8192
FFW = 14336
RANK = 512
N = 8
ROWS = 28
PAD = 32
HALF = 16
MESH = pl.DeviceIdType.MESH
HIGHEST = lax.Precision.HIGHEST
VMEM = pl.BlockSpec(memory_space=pltpu.VMEM)


def params(collective_id):
    return pltpu.CompilerParams(
        collective_id=collective_id, has_side_effects=True, vmem_limit_bytes=48 * 2**20
    )


def wrap(index):
    return lax.rem(index + 2 * N, N)


def greet_start(peers):
    barrier = pltpu.get_barrier_semaphore()
    for peer in peers:
        pl.semaphore_signal(barrier, inc=1, device_id=peer, device_id_type=MESH)


def greet_end(peers):
    pl.semaphore_wait(pltpu.get_barrier_semaphore(), len(peers))


def remote(src, dst, send_sem, recv_sem, device):
    return pltpu.make_async_remote_copy(
        src_ref=src, dst_ref=dst, send_sem=send_sem, recv_sem=recv_sem,
        device_id=device, device_id_type=MESH,
    )


def place():
    fsdp = lax.axis_index("fsdp")
    return fsdp // N, lax.rem(fsdp, N), lax.axis_index("tp")


def line_device(axis, offset):
    y, z, tp = place()
    if axis == 0:
        return (wrap(y + offset) * N + z, tp)
    return (y * N + wrap(z + offset), tp)


def tp_device(offset):
    return (lax.axis_index("fsdp"), wrap(lax.axis_index("tp") + offset))


def all_peers():
    plane = [line_device(axis, k) for axis in range(2) for k in range(1, N)]
    return plane + [tp_device(k) for k in range(1, N)]


HALVES = (pl.ds(0, N // 2), pl.ds(N // 2, N // 2))
CHAINS = [(h, d, p) for q in range(2) for h in range(2) for d in range(2) for p in [d ^ q]]


def chain_length(direction, part):
    return N // 2 if direction == part else N // 2 - 1


def signs(direction):
    return 1 - 2 * direction


def arrived(ref, sem, spare, device):
    remote(ref, ref, spare, sem, device).wait_recv()


def left_here(ref, sem, spare, device):
    remote(ref, ref, sem, spare, device).wait_send()


def exchange(source, target, send_sem, recv_sem, devices):
    for i, device in enumerate(devices):
        remote(source(i), target(i), send_sem, recv_sem, device).start()


def gather_plane(mine, out, sends, direct, landing, visit):
    y, z, _ = place()
    ring, across = (y, z), (z, y)
    for k in range(1, N):
        for h in range(2):
            remote(
                mine.at[h], out.at[h, ring[h], across[h]], sends.at[0], direct.at[h],
                line_device(1 - h, k),
            ).start()
    for h in range(2):
        out[h, ring[h], across[h]] = mine[h]
    for h in range(2):
        arrived(
            out.at[h, ring[h], pl.ds(0, N - 1)], direct.at[h], sends.at[0], line_device(1 - h, 1)
        )
    arriving = {}
    device = line_device(0, 1)
    for step in range(1, N // 2 + 2):
        for h, d, p in CHAINS:
            if step == 1 and (h, d, p) == CHAINS[4]:
                for i, q in [(0, 0), (0, 1), (1, 0), (1, 1)]:
                    visit(i, ring[i], q)
                left_here(out.at[:, 0], sends.at[2], direct.at[0], device)
            if 1 < step <= chain_length(d, p) + 1:
                arriving[h, d, p].wait_recv()
            if step <= chain_length(d, p):
                ref = out.at[h, wrap(ring[h] - signs(d) * (step - 1)), HALVES[p]]
                arriving[h, d, p] = remote(
                    ref, ref, sends.at[2 if step == 1 and d == p else 1],
                    landing.at[h, d, p, step - 1], line_device(h, signs(d)),
                )
                arriving[h, d, p].start()
        for h, d, p in CHAINS:
            if 1 < step <= chain_length(d, p) + 1:
                visit(h, wrap(ring[h] - signs(d) * (step - 1)), p)
    left_here(out.at[:, 0, pl.ds(0, N - 1)], sends.at[0], direct.at[0], device)
    left_here(out.at[:, pl.ds(0, N - 2)], sends.at[1], direct.at[0], device)


def gather_sems():
    return [
        pltpu.SemaphoreType.DMA((3,)),
        pltpu.SemaphoreType.DMA((2,)),
        pltpu.SemaphoreType.DMA((2, 2, 2, N // 2)),
    ]


def front_kernel(
    factor_ref, wide_ref, left_ref, gram_ref,
    got, partial_ref, landed, local, first, second, mine, slice_ref,
    gather_sends, direct, landing, sends, recvs,
):
    y, z, tp = place()
    greet_start(all_peers())
    partial_ref[...] = jnp.zeros_like(partial_ref)
    greet_end(all_peers())

    def add_terms(h, index, part):
        block = wide_ref[h, index, HALVES[part]].reshape(N // 2 * HALF, wide_ref.shape[-1])
        rows = got[h, index, HALVES[part]].reshape(N // 2 * HALF, RANK)
        partial_ref[...] += lax.dot_general(
            block, rows, (((0,), (0,)), ((), ())), preferred_element_type=jnp.float32
        )

    gather_plane(factor_ref, got, gather_sends, direct, landing, add_terms)

    def rows(index):
        return pl.ds(pl.multiple_of(index * HALF, HALF), HALF)

    others = [tp_device(k) for k in range(1, N)]
    exchange(
        lambda i: partial_ref.at[rows(wrap(tp + i + 1))], lambda i: landed.at[i],
        sends.at[0], recvs.at[0], others,
    )
    arrived(landed, recvs.at[0], sends.at[0], others[0])
    total = partial_ref[rows(tp), :]
    for i in range(N - 1):
        total = total + landed[i]
    left_ref[rows(tp), :] = total
    exchange(
        lambda i: left_ref.at[rows(tp)], lambda i: left_ref.at[rows(tp)],
        sends.at[1], recvs.at[1], others,
    )
    most = left_ref.at[pl.ds(0, (N - 1) * HALF)]
    arrived(most, recvs.at[1], sends.at[1], others[0])

    size = RANK // N
    at = pl.ds(pl.multiple_of(tp // 2 * BLOCK, BLOCK), BLOCK)
    local[...] = full_dot(left_ref[:, at], left_ref[...], ((0,), (0,)))
    start = lax.rem(tp, 2) * size
    width = RANK // 2
    ring, across = (y, z), (z, y)

    def piece(index, base=0):
        return pl.ds(pl.multiple_of(base + index * N, N), N)

    def lanes(h):
        return pl.ds(h * width, width)

    along = [[line_device(axis, k) for k in range(1, N)] for axis in range(2)]
    for h in range(2):
        exchange(
            lambda i: local.at[piece(wrap(across[h] + i + 1), start), lanes(h)],
            lambda i: first.at[h, i], sends.at[2], recvs.at[2 + h], along[1 - h],
        )
    for h in range(2):
        arrived(first.at[h], recvs.at[2 + h], sends.at[2], others[0])
        total = local[piece(across[h], start), h * width : (h + 1) * width]
        for i in range(N - 1):
            total = total + first[h, i]
        mine[h] = total
        second[h, ring[h]] = total
        exchange(
            lambda i: mine.at[h], lambda i: second.at[h, ring[h]],
            sends.at[3], recvs.at[4 + h], along[h],
        )
    for h in range(2):
        arrived(second.at[h, pl.ds(0, N - 1)], recvs.at[4 + h], sends.at[3], others[0])
        total = second[h, 0]
        for k in range(1, N):
            total = total + second[h, k]
        slice_ref[piece(across[h]), h * width : (h + 1) * width] = total
        ref = slice_ref.at[piece(across[h]), lanes(h)]
        exchange(lambda i: ref, lambda i: ref, sends.at[4], recvs.at[6 + h], along[1 - h])
    some = pl.ds(0, (N - 1) * N)
    for h in range(2):
        arrived(slice_ref.at[some, lanes(h)], recvs.at[6 + h], sends.at[4], others[0])

    sibling = (lax.axis_index("fsdp"), tp + 1 - 2 * lax.rem(tp, 2))

    def slab(index, begin=0, count=size):
        begin = pl.multiple_of(wrap(index) * size + begin, size // 2)
        return gram_ref.at[pl.ds(begin, count)]

    far = []
    for d in range(2):
        far.append(
            remote(slice_ref, slab(tp), sends.at[5], recvs.at[8 + d], tp_device(2 * signs(d)))
        )
        far[d].start()
    remote(slice_ref, slab(tp), sends.at[5], recvs.at[12], sibling).start()
    gram_ref[pl.ds(pl.multiple_of(tp * size, size), size), :] = slice_ref[...]
    half = []
    for d in range(2):
        far[d].wait_recv()
        ref = slab(tp - 2 * signs(d), d * (size // 2), size // 2)
        half.append(remote(ref, ref, sends.at[5], recvs.at[10 + d], tp_device(2 * signs(d))))
        half[d].start()
        ref = slab(tp - 2 * signs(d))
        remote(ref, ref, sends.at[5], recvs.at[12], sibling).start()
    for d in range(2):
        half[d].wait_recv()
    ref = slab(tp + N // 2)
    remote(ref, ref, sends.at[5], recvs.at[12], sibling).start()
    arrived(gram_ref.at[pl.ds(0, N // 2 * size)], recvs.at[12], sends.at[5], sibling)

    left_here(landed, sends.at[0], recvs.at[0], sibling)
    left_here(most, sends.at[1], recvs.at[0], sibling)
    left_here(first, sends.at[2], recvs.at[0], sibling)
    left_here(second.at[:, pl.ds(0, N - 1)], sends.at[3], recvs.at[0], sibling)
    left_here(slice_ref.at[some], sends.at[4], recvs.at[0], sibling)
    left_here(gram_ref.at[pl.ds(0, (N - 1) * size)], sends.at[5], recvs.at[0], sibling)


def front(factor, wide):
    rows = wide.shape[-1]
    f32 = jnp.float32
    return pl.pallas_call(
        front_kernel,
        out_shape=(
            jax.ShapeDtypeStruct((rows, RANK), f32),
            jax.ShapeDtypeStruct((RANK, RANK), f32),
        ),
        in_specs=[VMEM, VMEM],
        out_specs=(VMEM, VMEM),
        scratch_shapes=[
            pltpu.VMEM((2, N, N, HALF, RANK), jnp.bfloat16),
            pltpu.VMEM((rows, RANK), f32),
            pltpu.VMEM((N - 1, HALF, RANK), f32),
            pltpu.VMEM((BLOCK, RANK), f32),
            pltpu.VMEM((2, N - 1, N, RANK // 2), f32),
            pltpu.VMEM((2, N, N, RANK // 2), f32),
            pltpu.VMEM((2, N, RANK // 2), f32),
            pltpu.VMEM((RANK // N, RANK), f32),
        ]
        + gather_sems()
        + [pltpu.SemaphoreType.DMA((6,)), pltpu.SemaphoreType.DMA((13,))],
        compiler_params=params(0),
        name="front",
    )(factor, wide)


BLOCK = 128
BASE = 8


def small_inverse(panel, first):
    wide = (BASE, BLOCK)
    entry = {
        (i, j): jnp.broadcast_to(panel[i : i + 1, first + j : first + j + 1], wide)
        for i in range(BASE)
        for j in range(i + 1)
    }
    lower, inverse, scale = {}, {}, {}
    for j in range(BASE):
        pivot = entry[j, j]
        guess = lax.rsqrt(pivot)
        scale[j] = guess * (1.5 - 0.5 * ((pivot * guess) * guess))
        for i in range(j + 1, BASE):
            lower[i, j] = entry[i, j] * scale[j]
        for i in range(j + 1, BASE):
            for m in range(j + 1, i + 1):
                entry[i, m] = entry[i, m] - lower[i, j] * lower[m, j]
    for j in range(BASE):
        inverse[j, j] = scale[j]
        for i in range(j + 1, BASE):
            total = lower[i, j] * inverse[j, j]
            for m in range(j + 1, i):
                total = total + lower[i, m] * inverse[m, j]
            inverse[i, j] = -(scale[i] * total)
    index = lax.broadcasted_iota(jnp.int32, wide, 0)
    columns, rows = [], []
    for j in range(BASE):
        column = jnp.zeros(wide, jnp.float32)
        row = jnp.zeros(wide, jnp.float32)
        for i in range(j, BASE):
            column = jnp.where(index == i, inverse[i, j], column)
        for i in range(j + 1):
            row = jnp.where(index == i, inverse[j, i], row)
        columns.append(column)
        rows.append(row)
    return columns, rows


def add_up(terms):
    while len(terms) > 1:
        terms = [sum(terms[i + 1 : i + 2], terms[i]) for i in range(0, len(terms), 2)]
    return terms[0]


def combine(factors, panel):
    return [
        add_up([factors[m] * piece[m : m + 1, :] for m in range(BASE)]) for piece in panel
    ]


def block_inverse(block):
    row = lax.broadcasted_iota(jnp.int32, (BLOCK, BLOCK), 0)
    column = lax.broadcasted_iota(jnp.int32, (BLOCK, BLOCK), 1)
    unit = jnp.where(row == column, 1.0, 0.0).astype(jnp.float32)
    count = BLOCK // BASE
    panels = [
        [matrix[b * BASE : (b + 1) * BASE, :] for matrix in (block, unit)] for b in range(count)
    ]
    solved = []
    for b in range(count):
        first = b * BASE
        columns, rows = small_inverse(panels[b][0], first)
        done = combine(columns, panels[b])
        solved.append(done[1])
        if b + 1 == count:
            break
        again = combine(rows, done)
        ahead = panels[b + 1]
        factors = [
            jnp.broadcast_to(ahead[0][:, first + m : first + m + 1], (BASE, BLOCK))
            for m in range(BASE)
        ]
        panels[b + 1] = [old - new for old, new in zip(ahead, combine(factors, again))]
        if b + 2 == count:
            continue
        multiplier = jnp.concatenate([panels[c][0] for c in range(b + 2, count)], axis=0)
        parts = [jnp.concatenate(again, axis=1)]
        parts.append(jnp.zeros((BLOCK - first - BASE, 2 * BLOCK), jnp.float32))
        if first:
            parts.insert(0, jnp.zeros((first, 2 * BLOCK), jnp.float32))
        change = jnp.dot(
            multiplier, jnp.concatenate(parts, axis=0), precision=HIGHEST,
            preferred_element_type=jnp.float32,
        )
        for c in range(b + 2, count):
            at = (c - b - 2) * BASE
            panels[c] = [
                old - change[at : at + BASE, i * BLOCK : (i + 1) * BLOCK]
                for i, old in enumerate(panels[c])
            ]
    return jnp.where(row >= column, jnp.concatenate(solved, axis=0), 0.0)


def full_dot(x, y, dims):
    return lax.dot_general(
        x, y, (dims, ((), ())), precision=HIGHEST, preferred_element_type=jnp.float32
    )


def ortho_kernel(gram_ref, left_ref, out_ref, rest, tail):
    rest[...] = gram_ref[...]
    tail[...] = left_ref[...]
    for at in range(0, RANK, BLOCK):
        end = at + BLOCK
        inverse = block_inverse(rest[at:end, at:end])
        done = full_dot(tail[:, at:end], inverse, ((1,), (1,)))
        out_ref[:, at:end] = done.astype(out_ref.dtype)
        if end == RANK:
            break
        panel = full_dot(inverse, rest[at:end, end:], ((1,), (0,)))
        for start in range(end, RANK, BLOCK):
            piece = panel[:, start - end : start - end + BLOCK]
            rest[start : start + BLOCK, start:] -= full_dot(
                piece, panel[:, start - end :], ((0,), (0,))
            )
        tail[:, end:] -= full_dot(done, panel, ((1,), (0,)))


def orthonormalize(gram, left):
    return pl.pallas_call(
        ortho_kernel,
        out_shape=jax.ShapeDtypeStruct(left.shape, jnp.bfloat16),
        in_specs=[VMEM, VMEM],
        out_specs=VMEM,
        scratch_shapes=[
            pltpu.VMEM((RANK, RANK), jnp.float32),
            pltpu.VMEM(left.shape, jnp.float32),
        ],
        compiler_params=pltpu.CompilerParams(vmem_limit_bytes=48 * 2**20),
        name="orthonormalize",
    )(gram, left)


LINKS = N // 2 + 1


def right_kernel(
    wide_ref, ortho_ref, mine_ref, right_ref, squares_ref,
    chain, terms, summed, landed, squares, spread,
    gather_sends, direct, landing, sends, chain_recv, recvs,
):
    y, z, tp = place()
    ring, across = (y, z), (z, y)
    greet_start(all_peers())

    def own(h, target, part):
        block = wide_ref[h, wrap(target), HALVES[part]]
        product = jnp.dot(
            block.reshape(N // 2 * HALF, block.shape[-1]), ortho_ref[...],
            preferred_element_type=jnp.float32,
        )
        return product.reshape(N // 2, HALF, RANK)

    arriving = {}

    def slot(h, d, p, step):
        return chain.at[h, LINKS * d + step, HALVES[p]]

    def pass_on(h, d, p, step):
        arriving[h, d, p] = remote(
            slot(h, d, p, step - 1), slot(h, d, p, step),
            sends.at[3 if step == 1 and d == p else 0], chain_recv.at[h, d, p, step - 1],
            line_device(h, signs(d)),
        )
        arriving[h, d, p].start()

    def prepare(step):
        for h, d, p in CHAINS:
            if step < chain_length(d, p):
                target = ring[h] + signs(d) * (chain_length(d, p) - step)
                terms[h, d, HALVES[p]] = own(h, target, p)

    for h, d, p in CHAINS:
        term = own(h, ring[h] + signs(d) * chain_length(d, p), p)
        slot(h, d, p, 0)[...] = term.astype(jnp.bfloat16)
    squares[...] = jnp.zeros_like(squares)
    greet_end(all_peers())
    device = line_device(0, 1)
    for h, d, p in CHAINS[:4]:
        pass_on(h, d, p, 1)
    prepare(1)
    left_here(chain.at[:, 0], sends.at[3], recvs.at[0], device)
    for h, d, p in CHAINS[4:]:
        pass_on(h, d, p, 1)
    for step in range(1, N // 2):
        for h, d, p in CHAINS:
            if step < chain_length(d, p):
                arriving[h, d, p].wait_recv()
                ref = slot(h, d, p, step)
                total = terms[h, d, HALVES[p]] + ref[...].astype(jnp.float32)
                ref[...] = total.astype(jnp.bfloat16)
                pass_on(h, d, p, step + 1)
        prepare(step + 1)
    for h, d, p in CHAINS[4:]:
        arriving[h, d, p].wait_recv()
        ref = slot(h, d, p, chain_length(d, p))
        terms[h, 0, HALVES[p]] = own(h, ring[h], p) + ref[...].astype(jnp.float32)
    for h in range(2):
        for i, d, p in CHAINS[:4]:
            if i == h:
                arriving[h, d, p].wait_recv()
                ref = slot(h, d, p, chain_length(d, p))
                total = terms[h, 0, HALVES[p]] + ref[...].astype(jnp.float32)
                summed[h, HALVES[p]] = total.astype(jnp.bfloat16)
        exchange(
            lambda i: summed.at[h, wrap(across[h] + i + 1)], lambda i: landed.at[h, i],
            sends.at[1], recvs.at[h], [line_device(1 - h, k) for k in range(1, N)],
        )
    for h in range(2):
        arrived(landed.at[h], recvs.at[h], sends.at[1], device)
        total = summed[h, across[h]].astype(jnp.float32)
        for i in range(N - 1):
            total = total + landed[h, i].astype(jnp.float32)
        mine_ref[h] = total.astype(jnp.bfloat16)

    def add_squares(h, index, part):
        block = right_ref[h, index, HALVES[part]].astype(jnp.float32)
        block = block.reshape(HALF // 2, N, RANK)
        squares[...] += jnp.sum(block * block, axis=0)

    gather_plane(mine_ref, right_ref, gather_sends, direct, landing, add_squares)

    exchange(
        lambda i: squares, lambda i: spread.at[tp], sends.at[2], recvs.at[2],
        [tp_device(k) for k in range(1, N)],
    )
    spread[tp] = squares[...]
    others = spread.at[pl.ds(0, N - 1)]
    arrived(others, recvs.at[2], sends.at[2], device)
    total = spread[0]
    for k in range(1, N):
        total = total + spread[k]
    squares_ref[...] = total
    left_here(chain.at[:, pl.ds(0, N - 2)], sends.at[0], recvs.at[0], device)
    left_here(landed, sends.at[1], recvs.at[0], device)
    left_here(others, sends.at[2], recvs.at[0], device)


def make_right(wide, ortho):
    f32, bf16 = jnp.float32, jnp.bfloat16
    return pl.pallas_call(
        right_kernel,
        out_shape=(
            jax.ShapeDtypeStruct((2, HALF, RANK), bf16),
            jax.ShapeDtypeStruct((2, N, N, HALF, RANK), bf16),
            jax.ShapeDtypeStruct((N, RANK), f32),
        ),
        in_specs=[VMEM] * 2,
        out_specs=(VMEM,) * 3,
        scratch_shapes=[
            pltpu.VMEM((2, 2 * LINKS, N, HALF, RANK), bf16),
            pltpu.VMEM((2, 2, N, HALF, RANK), f32),
            pltpu.VMEM((2, N, HALF, RANK), bf16),
            pltpu.VMEM((2, N - 1, HALF, RANK), bf16),
            pltpu.VMEM((N, RANK), f32),
            pltpu.VMEM((N, N, RANK), f32),
        ]
        + gather_sems()
        + [
            pltpu.SemaphoreType.DMA((4,)),
            pltpu.SemaphoreType.DMA((2, 2, 2, N // 2)),
            pltpu.SemaphoreType.DMA((3,)),
        ],
        compiler_params=params(1),
        name="make_right",
    )(wide, ortho)


def finish_kernel(
    squares_ref, first_ref, second_ref, mine_ref, ortho_ref, gradient_ref, momentum_ref,
    update_ref, new_ref, factor_ref, factor,
):
    squares = jnp.sum(squares_ref[...], axis=0, keepdims=True)
    norms = jnp.sqrt(squares + 1e-06)
    gain = math.sqrt(FFW) / norms
    ortho = ortho_ref[...]
    scaled = (ortho.astype(jnp.float32) * (norms / math.sqrt(FFW))).astype(jnp.bfloat16)
    stacked = jnp.concatenate([ortho, scaled], axis=0)
    group = 4

    def joined(top, bottom):
        top = top.astype(jnp.float32) * gain
        bottom = bottom.astype(jnp.float32) * gain
        return [top, bottom[: ROWS - HALF]]

    factor_ref[...] = jnp.concatenate(joined(mine_ref[0], mine_ref[1]), axis=0).astype(jnp.bfloat16)
    for y in range(first_ref.shape[1]):
        for z in range(0, N, group):
            pieces = []
            for i in range(z, z + group):
                pieces += joined(first_ref[0, y, i], second_ref[0, i, y])
            start = (y * N + z) * ROWS
            factor[start : start + group * ROWS, :] = jnp.concatenate(
                pieces, axis=0
            ).astype(jnp.bfloat16)
    combined = lax.dot_general(
        stacked, factor[...], (((1,), (1,)), ((), ())), preferred_element_type=jnp.float32
    )
    rows = ortho.shape[0]
    update_ref[...] = (math.sqrt(D / RANK) * combined[:rows]).astype(jnp.bfloat16)
    whole = momentum_ref[...] + gradient_ref[...].astype(jnp.float32)
    new_ref[...] = whole - 0.05 * combined[rows:]


def finish(squares, right, mine, ortho, gradient, momentum):
    steps = 2
    rows, columns = gradient.shape
    some = N // steps
    whole = lambda *shape: pl.BlockSpec(shape, lambda i: (0,) * len(shape))
    tile = pl.BlockSpec((rows, columns // steps), lambda i: (0, i))
    return pl.pallas_call(
        finish_kernel,
        grid=(steps,),
        out_shape=(
            jax.ShapeDtypeStruct((rows, columns), jnp.bfloat16),
            jax.ShapeDtypeStruct((rows, columns), jnp.float32),
            jax.ShapeDtypeStruct((ROWS, RANK), jnp.bfloat16),
        ),
        in_specs=[
            whole(N, RANK),
            pl.BlockSpec((1, some, N, HALF, RANK), lambda i: (0, i, 0, 0, 0)),
            pl.BlockSpec((1, N, some, HALF, RANK), lambda i: (1, 0, i, 0, 0)),
            whole(2, HALF, RANK),
            whole(rows, RANK),
            tile,
            tile,
        ],
        out_specs=(tile, tile, whole(ROWS, RANK)),
        scratch_shapes=[pltpu.VMEM((columns // steps, RANK), jnp.bfloat16)],
        compiler_params=pltpu.CompilerParams(vmem_limit_bytes=48 * 2**20),
        name="finish",
    )(squares, right, right, mine, ortho, gradient, momentum)


def body(gradient, momentum, right_factor):
    wide = (momentum + gradient.astype(jnp.float32)).astype(jnp.bfloat16)
    row_count = wide.shape[0]
    blocks = wide.T.reshape(N, N, ROWS, row_count)
    blocks = jnp.pad(blocks, ((0, 0), (0, 0), (0, PAD - ROWS), (0, 0)))
    blocks = jnp.stack([blocks[:, :, :HALF], jnp.swapaxes(blocks[:, :, HALF:], 0, 1)])
    factor = jnp.pad(right_factor, ((0, PAD - ROWS), (0, 0))).reshape(2, HALF, RANK)
    left, gram = front(factor, blocks)
    ortho = orthonormalize(gram, left)
    mine, right, squares = make_right(blocks, ortho)
    return finish(squares, right, mine, ortho, gradient, momentum)


def solution(mesh):
    return jax.shard_map(
        body,
        mesh=mesh,
        in_specs=(P("fsdp", "tp"), P("fsdp", "tp"), P(("tp", "fsdp"), None)),
        out_specs=(P("fsdp", "tp"), P("fsdp", "tp"), P(("tp", "fsdp"), None)),
        check_vma=False,
    )
```

```python
import functools
import math

import jax
import jax.numpy as jnp
from jax import lax
from jax.experimental import pallas as pl
from jax.experimental.pallas import tpu as pltpu
from jax.sharding import PartitionSpec as P

D = 8192
FFW = 14336
RANK = 512
N = 8
ROWS = 28
PAD = 32
HALF = 16
BLOCK = 128
MESH = pl.DeviceIdType.MESH
HIGHEST = lax.Precision.HIGHEST
VMEM = pl.BlockSpec(memory_space=pltpu.VMEM)


def params(collective_id):
    return pltpu.CompilerParams(
        collective_id=collective_id, has_side_effects=True, vmem_limit_bytes=48 * 2**20
    )


def wrap(index):
    return lax.rem(index + 2 * N, N)


def greet_start(peers):
    barrier = pltpu.get_barrier_semaphore()
    for peer in peers:
        pl.semaphore_signal(barrier, inc=1, device_id=peer, device_id_type=MESH)


def greet_end(peers):
    pl.semaphore_wait(pltpu.get_barrier_semaphore(), len(peers))


def remote(src, dst, send_sem, recv_sem, device):
    return pltpu.make_async_remote_copy(
        src_ref=src, dst_ref=dst, send_sem=send_sem, recv_sem=recv_sem,
        device_id=device, device_id_type=MESH,
    )


def place():
    fsdp = lax.axis_index("fsdp")
    return fsdp // N, lax.rem(fsdp, N), lax.axis_index("tp")


def line_device(axis, offset):
    y, z, tp = place()
    if axis == 0:
        return (wrap(y + offset) * N + z, tp)
    return (y * N + wrap(z + offset), tp)


def split(rows):
    rest = jnp.concatenate(
        [rows[HALF:], jnp.zeros((PAD - ROWS, rows.shape[1]), jnp.float32)], axis=0
    )
    return rows[:HALF].astype(jnp.bfloat16), rest.astype(jnp.bfloat16)


def tp_device(offset):
    return (lax.axis_index("fsdp"), wrap(lax.axis_index("tp") + offset))


def all_peers():
    plane = [line_device(axis, k) for axis in range(2) for k in range(1, N)]
    return plane + [tp_device(k) for k in range(1, N)]


HALVES = (pl.ds(0, N // 2), pl.ds(N // 2, N // 2))
CHAINS = [(h, d, p) for q in range(2) for h in range(2) for d in range(2) for p in [d ^ q]]


def chain_length(direction, part):
    return N // 2 if direction == part else N // 2 - 1


def signs(direction):
    return 1 - 2 * direction


def arrived(ref, sem, spare, device):
    remote(ref, ref, spare, sem, device).wait_recv()


def left_here(ref, sem, spare, device):
    remote(ref, ref, sem, spare, device).wait_send()


def exchange(source, target, send_sem, recv_sem, devices):
    for i, device in enumerate(devices):
        remote(source(i), target(i), send_sem, recv_sem, device).start()


def gather_plane(mine, out, sends, direct, landing, visit=None, beside=None):
    y, z, _ = place()
    ring, across = (y, z), (z, y)
    for k in range(1, N):
        for h in range(2):
            remote(
                mine.at[h], out.at[h, ring[h], across[h]], sends.at[0], direct.at[h],
                line_device(1 - h, k),
            ).start()
    for h in range(2):
        out[h, ring[h], across[h]] = mine[h]
    if beside is not None:
        beside(0)
    for h in range(2):
        arrived(
            out.at[h, ring[h], pl.ds(0, N - 1)], direct.at[h], sends.at[0], line_device(1 - h, 1)
        )
    arriving = {}
    device = line_device(0, 1)
    for step in range(1, N // 2 + 2):
        for h, d, p in CHAINS:
            if step == 1 and (h, d, p) == CHAINS[4]:
                if visit is not None:
                    for i, q in [(0, 0), (0, 1), (1, 0), (1, 1)]:
                        visit(i, ring[i], q)
                if beside is not None:
                    beside(1)
                left_here(out.at[:, 0], sends.at[2], direct.at[0], device)
            if 1 < step <= chain_length(d, p) + 1:
                arriving[h, d, p].wait_recv()
            if step <= chain_length(d, p):
                ref = out.at[h, wrap(ring[h] - signs(d) * (step - 1)), HALVES[p]]
                arriving[h, d, p] = remote(
                    ref, ref, sends.at[2 if step == 1 and d == p else 1],
                    landing.at[h, d, p, step - 1], line_device(h, signs(d)),
                )
                arriving[h, d, p].start()
        if visit is not None:
            for h, d, p in CHAINS:
                if 1 < step <= chain_length(d, p) + 1:
                    visit(h, wrap(ring[h] - signs(d) * (step - 1)), p)
        if beside is not None and step > 1:
            beside(step)
    left_here(out.at[:, 0, pl.ds(0, N - 1)], sends.at[0], direct.at[0], device)
    left_here(out.at[:, pl.ds(0, N - 2)], sends.at[1], direct.at[0], device)


def gather_sems():
    return [
        pltpu.SemaphoreType.DMA((3,)),
        pltpu.SemaphoreType.DMA((2,)),
        pltpu.SemaphoreType.DMA((2, 2, 2, N // 2)),
    ]


def front_part(
    factor_ref, gradient_ref, momentum_ref, left_ref, gram_ref, wide_ref,
    turned, got, partial_ref, landed, local, first, second, mine, slice_ref, padded,
    gather_sends, direct, landing, sends, recvs,
):
    y, z, tp = place()
    greet_start(all_peers())
    partial_ref[...] = jnp.zeros_like(partial_ref)
    padded[0], padded[1] = split(factor_ref[...].astype(jnp.float32))
    greet_end(all_peers())

    def arrange(step):
        if step:
            return
        wide = (momentum_ref[...] + gradient_ref[...].astype(jnp.float32)).astype(jnp.bfloat16)
        turned[...] = wide.astype(jnp.float32).T
        for i in range(N):
            for j in range(N):
                at = (i * N + j) * ROWS
                wide_ref[0, i, j], wide_ref[1, j, i] = split(turned[at : at + ROWS, :])

    def add_terms(h, index, part):
        block = wide_ref[h, index, HALVES[part]].reshape(N // 2 * HALF, wide_ref.shape[-1])
        rows = got[h, index, HALVES[part]].reshape(N // 2 * HALF, RANK)
        partial_ref[...] += lax.dot_general(
            block, rows, (((0,), (0,)), ((), ())), preferred_element_type=jnp.float32
        )

    gather_plane(padded, got, gather_sends, direct, landing, add_terms, arrange)

    def rows(index):
        return pl.ds(pl.multiple_of(index * HALF, HALF), HALF)

    others = [tp_device(k) for k in range(1, N)]
    exchange(
        lambda i: partial_ref.at[rows(wrap(tp + i + 1))], lambda i: landed.at[i],
        sends.at[0], recvs.at[0], others,
    )
    arrived(landed, recvs.at[0], sends.at[0], others[0])
    total = partial_ref[rows(tp), :]
    for i in range(N - 1):
        total = total + landed[i]
    left_ref[rows(tp), :] = total
    exchange(
        lambda i: left_ref.at[rows(tp)], lambda i: left_ref.at[rows(tp)],
        sends.at[1], recvs.at[1], others,
    )
    most = left_ref.at[pl.ds(0, (N - 1) * HALF)]
    arrived(most, recvs.at[1], sends.at[1], others[0])

    size = RANK // N
    at = pl.ds(pl.multiple_of(tp // 2 * BLOCK, BLOCK), BLOCK)
    local[...] = full_dot(left_ref[:, at], left_ref[...], ((0,), (0,)))
    start = lax.rem(tp, 2) * size
    width = RANK // 2
    ring, across = (y, z), (z, y)

    def piece(index, base=0):
        return pl.ds(pl.multiple_of(base + index * N, N), N)

    def lanes(h):
        return pl.ds(h * width, width)

    along = [[line_device(axis, k) for k in range(1, N)] for axis in range(2)]
    for h in range(2):
        exchange(
            lambda i: local.at[piece(wrap(across[h] + i + 1), start), lanes(h)],
            lambda i: first.at[h, i], sends.at[2], recvs.at[2 + h], along[1 - h],
        )
    for h in range(2):
        arrived(first.at[h], recvs.at[2 + h], sends.at[2], others[0])
        total = local[piece(across[h], start), h * width : (h + 1) * width]
        for i in range(N - 1):
            total = total + first[h, i]
        mine[h] = total
        second[h, ring[h]] = total
        exchange(
            lambda i: mine.at[h], lambda i: second.at[h, ring[h]],
            sends.at[3], recvs.at[4 + h], along[h],
        )
    for h in range(2):
        arrived(second.at[h, pl.ds(0, N - 1)], recvs.at[4 + h], sends.at[3], others[0])
        total = second[h, 0]
        for k in range(1, N):
            total = total + second[h, k]
        slice_ref[piece(across[h]), h * width : (h + 1) * width] = total
        ref = slice_ref.at[piece(across[h]), lanes(h)]
        exchange(lambda i: ref, lambda i: ref, sends.at[4], recvs.at[6 + h], along[1 - h])
    some = pl.ds(0, (N - 1) * N)
    for h in range(2):
        arrived(slice_ref.at[some, lanes(h)], recvs.at[6 + h], sends.at[4], others[0])

    sibling = (lax.axis_index("fsdp"), tp + 1 - 2 * lax.rem(tp, 2))

    def slab(index, begin=0, count=size):
        begin = pl.multiple_of(wrap(index) * size + begin, size // 2)
        return gram_ref.at[pl.ds(begin, count)]

    far = []
    for d in range(2):
        far.append(
            remote(slice_ref, slab(tp), sends.at[5], recvs.at[8 + d], tp_device(2 * signs(d)))
        )
        far[d].start()
    remote(slice_ref, slab(tp), sends.at[5], recvs.at[12], sibling).start()
    gram_ref[pl.ds(pl.multiple_of(tp * size, size), size), :] = slice_ref[...]
    half = []
    for d in range(2):
        far[d].wait_recv()
        ref = slab(tp - 2 * signs(d), d * (size // 2), size // 2)
        half.append(remote(ref, ref, sends.at[5], recvs.at[10 + d], tp_device(2 * signs(d))))
        half[d].start()
        ref = slab(tp - 2 * signs(d))
        remote(ref, ref, sends.at[5], recvs.at[12], sibling).start()
    for d in range(2):
        half[d].wait_recv()
    ref = slab(tp + N // 2)
    remote(ref, ref, sends.at[5], recvs.at[12], sibling).start()
    arrived(gram_ref.at[pl.ds(0, N // 2 * size)], recvs.at[12], sends.at[5], sibling)

    left_here(landed, sends.at[0], recvs.at[0], sibling)
    left_here(most, sends.at[1], recvs.at[0], sibling)
    left_here(first, sends.at[2], recvs.at[0], sibling)
    left_here(second.at[:, pl.ds(0, N - 1)], sends.at[3], recvs.at[0], sibling)
    left_here(slice_ref.at[some], sends.at[4], recvs.at[0], sibling)
    left_here(gram_ref.at[pl.ds(0, (N - 1) * size)], sends.at[5], recvs.at[0], sibling)


BASE = 8


def small_inverse(panel, first):
    wide = (BASE, BLOCK)
    entry = {
        (i, j): jnp.broadcast_to(panel[i : i + 1, first + j : first + j + 1], wide)
        for i in range(BASE)
        for j in range(i + 1)
    }
    lower, inverse, scale = {}, {}, {}
    for j in range(BASE):
        pivot = entry[j, j]
        guess = lax.rsqrt(pivot)
        scale[j] = guess * (1.5 - 0.5 * ((pivot * guess) * guess))
        for i in range(j + 1, BASE):
            lower[i, j] = entry[i, j] * scale[j]
        for i in range(j + 1, BASE):
            for m in range(j + 1, i + 1):
                entry[i, m] = entry[i, m] - lower[i, j] * lower[m, j]
    for j in range(BASE):
        inverse[j, j] = scale[j]
        for i in range(j + 1, BASE):
            total = lower[i, j] * inverse[j, j]
            for m in range(j + 1, i):
                total = total + lower[i, m] * inverse[m, j]
            inverse[i, j] = -(scale[i] * total)
    index = lax.broadcasted_iota(jnp.int32, wide, 0)
    columns, rows = [], []
    for j in range(BASE):
        column = jnp.zeros(wide, jnp.float32)
        row = jnp.zeros(wide, jnp.float32)
        for i in range(j, BASE):
            column = jnp.where(index == i, inverse[i, j], column)
        for i in range(j + 1):
            row = jnp.where(index == i, inverse[j, i], row)
        columns.append(column)
        rows.append(row)
    return columns, rows


def add_up(terms):
    while len(terms) > 1:
        terms = [sum(terms[i + 1 : i + 2], terms[i]) for i in range(0, len(terms), 2)]
    return terms[0]


def combine(factors, panel):
    return [
        add_up([factors[m] * piece[m : m + 1, :] for m in range(BASE)]) for piece in panel
    ]


def block_inverse(block):
    row = lax.broadcasted_iota(jnp.int32, (BLOCK, BLOCK), 0)
    column = lax.broadcasted_iota(jnp.int32, (BLOCK, BLOCK), 1)
    unit = jnp.where(row == column, 1.0, 0.0).astype(jnp.float32)
    count = BLOCK // BASE
    panels = [
        [matrix[b * BASE : (b + 1) * BASE, :] for matrix in (block, unit)] for b in range(count)
    ]
    solved = []
    for b in range(count):
        first = b * BASE
        columns, rows = small_inverse(panels[b][0], first)
        done = combine(columns, panels[b])
        solved.append(done[1])
        if b + 1 == count:
            break
        again = combine(rows, done)
        ahead = panels[b + 1]
        factors = [
            jnp.broadcast_to(ahead[0][:, first + m : first + m + 1], (BASE, BLOCK))
            for m in range(BASE)
        ]
        panels[b + 1] = [old - new for old, new in zip(ahead, combine(factors, again))]
        if b + 2 == count:
            continue
        multiplier = jnp.concatenate([panels[c][0] for c in range(b + 2, count)], axis=0)
        parts = [jnp.concatenate(again, axis=1)]
        parts.append(jnp.zeros((BLOCK - first - BASE, 2 * BLOCK), jnp.float32))
        if first:
            parts.insert(0, jnp.zeros((first, 2 * BLOCK), jnp.float32))
        change = jnp.dot(
            multiplier, jnp.concatenate(parts, axis=0), precision=HIGHEST,
            preferred_element_type=jnp.float32,
        )
        for c in range(b + 2, count):
            at = (c - b - 2) * BASE
            panels[c] = [
                old - change[at : at + BASE, i * BLOCK : (i + 1) * BLOCK]
                for i, old in enumerate(panels[c])
            ]
    return jnp.where(row >= column, jnp.concatenate(solved, axis=0), 0.0)


def full_dot(x, y, dims):
    return lax.dot_general(
        x, y, (dims, ((), ())), precision=HIGHEST, preferred_element_type=jnp.float32
    )


def ortho_part(rest, tail, out_ref):
    for at in range(0, RANK, BLOCK):
        end = at + BLOCK
        inverse = block_inverse(rest[at:end, at:end])
        done = full_dot(tail[:, at:end], inverse, ((1,), (1,)))
        out_ref[:, at:end] = done.astype(out_ref.dtype)
        if end == RANK:
            break
        panel = full_dot(inverse, rest[at:end, end:], ((1,), (0,)))
        for start in range(end, RANK, BLOCK):
            piece = panel[:, start - end : start - end + BLOCK]
            rest[start : start + BLOCK, start:] -= full_dot(
                piece, panel[:, start - end :], ((0,), (0,))
            )
        tail[:, end:] -= full_dot(done, panel, ((1,), (0,)))


LINKS = N // 2 + 1


def right_part(
    wide_ref, ortho_ref, mine_ref, right_ref, squares_ref,
    chain, terms, summed, landed, squares, over_tp, over_line,
    gather_sends, direct, landing, sends, chain_recv, recvs,
):
    y, z, tp = place()
    ring, across = (y, z), (z, y)

    def own(h, target, part):
        block = wide_ref[h, wrap(target), HALVES[part]]
        product = jnp.dot(
            block.reshape(N // 2 * HALF, block.shape[-1]), ortho_ref[...],
            preferred_element_type=jnp.float32,
        )
        return product.reshape(N // 2, HALF, RANK)

    arriving = {}

    def slot(h, d, p, step):
        return chain.at[h, LINKS * d + step, HALVES[p]]

    def pass_on(h, d, p, step):
        arriving[h, d, p] = remote(
            slot(h, d, p, step - 1), slot(h, d, p, step),
            sends.at[3 if step == 1 and d == p else 0], chain_recv.at[h, d, p, step - 1],
            line_device(h, signs(d)),
        )
        arriving[h, d, p].start()

    def prepare(step):
        for h, d, p in CHAINS:
            if step < chain_length(d, p):
                target = ring[h] + signs(d) * (chain_length(d, p) - step)
                terms[h, d, HALVES[p]] = own(h, target, p)

    for h, d, p in CHAINS:
        term = own(h, ring[h] + signs(d) * chain_length(d, p), p)
        slot(h, d, p, 0)[...] = term.astype(jnp.bfloat16)
    device = line_device(0, 1)
    for h, d, p in CHAINS[:4]:
        pass_on(h, d, p, 1)
    prepare(1)
    left_here(chain.at[:, 0], sends.at[3], recvs.at[0], device)
    for h, d, p in CHAINS[4:]:
        pass_on(h, d, p, 1)
    for step in range(1, N // 2):
        for h, d, p in CHAINS:
            if step < chain_length(d, p):
                arriving[h, d, p].wait_recv()
                ref = slot(h, d, p, step)
                total = terms[h, d, HALVES[p]] + ref[...].astype(jnp.float32)
                ref[...] = total.astype(jnp.bfloat16)
                pass_on(h, d, p, step + 1)
        prepare(step + 1)
    for h, d, p in CHAINS[4:]:
        arriving[h, d, p].wait_recv()
        ref = slot(h, d, p, chain_length(d, p))
        terms[h, 0, HALVES[p]] = own(h, ring[h], p) + ref[...].astype(jnp.float32)
    for h in range(2):
        for i, d, p in CHAINS[:4]:
            if i == h:
                arriving[h, d, p].wait_recv()
                ref = slot(h, d, p, chain_length(d, p))
                total = terms[h, 0, HALVES[p]] + ref[...].astype(jnp.float32)
                summed[h, HALVES[p]] = total.astype(jnp.bfloat16)
        exchange(
            lambda i: summed.at[h, wrap(across[h] + i + 1)], lambda i: landed.at[h, i],
            sends.at[1], recvs.at[h], [line_device(1 - h, k) for k in range(1, N)],
        )
    for h in range(2):
        arrived(landed.at[h], recvs.at[h], sends.at[1], device)
        total = summed[h, across[h]].astype(jnp.float32)
        for i in range(N - 1):
            total = total + landed[h, i].astype(jnp.float32)
        mine_ref[h] = total.astype(jnp.bfloat16)

    def add_squares(step):
        if step == 1:
            for h in range(2):
                block = right_ref[h, ring[h]].astype(jnp.float32).reshape(N * HALF // N, N, RANK)
                total = jnp.sum(jnp.sum(block * block, axis=0), axis=0, keepdims=True)
                pieces = [total[:, c : c + BLOCK] for c in range(0, RANK, BLOCK)]
                pieces.append(jnp.zeros((N - len(pieces), BLOCK), jnp.float32))
                squares[h] = jnp.concatenate(pieces, axis=0)
            over_tp[tp] = squares[...]
            exchange(
                lambda i: squares, lambda i: over_tp.at[tp], sends.at[2], recvs.at[2],
                [tp_device(k) for k in range(1, N)],
            )
        if step == 3:
            arrived(over_tp.at[pl.ds(0, N - 1)], recvs.at[2], sends.at[2], device)
            total = over_tp[0]
            for k in range(1, N):
                total = total + over_tp[k]
            for h in range(2):
                over_line[h, ring[h]] = total[h]
                ref = over_line.at[h, ring[h]]
                exchange(
                    lambda i: ref, lambda i: ref, sends.at[4], recvs.at[3 + h],
                    [line_device(h, k) for k in range(1, N)],
                )

    gather_plane(
        mine_ref, right_ref, gather_sends, direct, landing, beside=add_squares
    )
    total = jnp.zeros((N, BLOCK), jnp.float32)
    for h in range(2):
        arrived(over_line.at[h, pl.ds(0, N - 1)], recvs.at[3 + h], sends.at[4], device)
        for k in range(N):
            total = total + over_line[h, k]
    squares_ref[...] = total
    left_here(chain.at[:, pl.ds(0, N - 2)], sends.at[0], recvs.at[0], device)
    left_here(landed, sends.at[1], recvs.at[0], device)
    left_here(over_tp.at[pl.ds(0, N - 1)], sends.at[2], recvs.at[0], device)
    left_here(over_line.at[:, pl.ds(0, N - 1)], sends.at[4], recvs.at[0], device)


FRONT_SCRATCH = [
    pltpu.VMEM((FFW // N, BLOCK), jnp.float32),
    pltpu.VMEM((2, N, N, HALF, RANK), jnp.bfloat16),
    pltpu.VMEM((BLOCK, RANK), jnp.float32),
    pltpu.VMEM((N - 1, HALF, RANK), jnp.float32),
    pltpu.VMEM((BLOCK, RANK), jnp.float32),
    pltpu.VMEM((2, N - 1, N, RANK // 2), jnp.float32),
    pltpu.VMEM((2, N, N, RANK // 2), jnp.float32),
    pltpu.VMEM((2, N, RANK // 2), jnp.float32),
    pltpu.VMEM((RANK // N, RANK), jnp.float32),
    pltpu.VMEM((2, HALF, RANK), jnp.bfloat16),
    *gather_sems(),
    pltpu.SemaphoreType.DMA((6,)),
    pltpu.SemaphoreType.DMA((13,)),
]


RIGHT_SCRATCH = [
    pltpu.VMEM((2, 2 * LINKS, N, HALF, RANK), jnp.bfloat16),
    pltpu.VMEM((2, 2, N, HALF, RANK), jnp.float32),
    pltpu.VMEM((2, N, HALF, RANK), jnp.bfloat16),
    pltpu.VMEM((2, N - 1, HALF, RANK), jnp.bfloat16),
    pltpu.VMEM((2, N, BLOCK), jnp.float32),
    pltpu.VMEM((N, 2, N, BLOCK), jnp.float32),
    pltpu.VMEM((2, N, N, BLOCK), jnp.float32),
    *gather_sems(),
    pltpu.SemaphoreType.DMA((5,)),
    pltpu.SemaphoreType.DMA((2, 2, 2, N // 2)),
    pltpu.SemaphoreType.DMA((5,)),
]


def step_kernel(
    factor_ref, gradient_ref, momentum_ref, ortho_ref, mine_ref, right_ref, squares_ref,
    left, gram, wide, *scratch,
):
    count = len(FRONT_SCRATCH)
    front_part(factor_ref, gradient_ref, momentum_ref, left, gram, wide, *scratch[:count])
    ortho_part(gram, left, ortho_ref)
    right_part(wide, ortho_ref, mine_ref, right_ref, squares_ref, *scratch[count:])


def make_right(factor, gradient, momentum):
    rows = gradient.shape[0]
    f32, bf16 = jnp.float32, jnp.bfloat16
    return pl.pallas_call(
        step_kernel,
        out_shape=(
            jax.ShapeDtypeStruct((rows, RANK), bf16),
            jax.ShapeDtypeStruct((2, HALF, RANK), bf16),
            jax.ShapeDtypeStruct((2, N, N, HALF, RANK), bf16),
            jax.ShapeDtypeStruct((N, BLOCK), f32),
        ),
        in_specs=[VMEM] * 3,
        out_specs=(VMEM,) * 4,
        scratch_shapes=[
            pltpu.VMEM((rows, RANK), f32),
            pltpu.VMEM((RANK, RANK), f32),
            pltpu.VMEM((2, N, N, HALF, rows), bf16),
        ]
        + FRONT_SCRATCH
        + RIGHT_SCRATCH,
        compiler_params=params(0),
        name="make_right",
    )(factor, gradient, momentum)


def finish_kernel(
    squares_ref, first_ref, second_ref, mine_ref, ortho_ref, gradient_ref, momentum_ref,
    update_ref, new_ref, factor_ref, factor,
):
    squares = jnp.concatenate([squares_ref[c : c + 1, :] for c in range(RANK // BLOCK)], axis=1)
    norms = jnp.sqrt(squares + 1e-06)
    gain = math.sqrt(FFW) / norms
    ortho = ortho_ref[...]
    scaled = (ortho.astype(jnp.float32) * (norms / math.sqrt(FFW))).astype(jnp.bfloat16)
    stacked = jnp.concatenate([ortho, scaled], axis=0)
    group = 4

    def joined(top, bottom):
        top = top.astype(jnp.float32) * gain
        bottom = bottom.astype(jnp.float32) * gain
        return [top, bottom[: ROWS - HALF]]

    factor_ref[...] = jnp.concatenate(joined(mine_ref[0], mine_ref[1]), axis=0).astype(jnp.bfloat16)
    for y in range(first_ref.shape[1]):
        for z in range(0, N, group):
            pieces = []
            for i in range(z, z + group):
                pieces += joined(first_ref[0, y, i], second_ref[0, i, y])
            start = (y * N + z) * ROWS
            factor[start : start + group * ROWS, :] = jnp.concatenate(
                pieces, axis=0
            ).astype(jnp.bfloat16)
    combined = lax.dot_general(
        stacked, factor[...], (((1,), (1,)), ((), ())), preferred_element_type=jnp.float32
    )
    rows = ortho.shape[0]
    update_ref[...] = (math.sqrt(D / RANK) * combined[:rows]).astype(jnp.bfloat16)
    whole = momentum_ref[...] + gradient_ref[...].astype(jnp.float32)
    new_ref[...] = whole - 0.05 * combined[rows:]


def finish(squares, right, mine, ortho, gradient, momentum):
    steps = 2
    rows, columns = gradient.shape
    some = N // steps
    whole = lambda *shape: pl.BlockSpec(shape, lambda i: (0,) * len(shape))
    tile = pl.BlockSpec((rows, columns // steps), lambda i: (0, i))
    return pl.pallas_call(
        finish_kernel,
        grid=(steps,),
        out_shape=(
            jax.ShapeDtypeStruct((rows, columns), jnp.bfloat16),
            jax.ShapeDtypeStruct((rows, columns), jnp.float32),
            jax.ShapeDtypeStruct((ROWS, RANK), jnp.bfloat16),
        ),
        in_specs=[
            whole(N, BLOCK),
            pl.BlockSpec((1, some, N, HALF, RANK), lambda i: (0, i, 0, 0, 0)),
            pl.BlockSpec((1, N, some, HALF, RANK), lambda i: (1, 0, i, 0, 0)),
            whole(2, HALF, RANK),
            whole(rows, RANK),
            tile,
            tile,
        ],
        out_specs=(tile, tile, whole(ROWS, RANK)),
        scratch_shapes=[pltpu.VMEM((columns // steps, RANK), jnp.bfloat16)],
        compiler_params=pltpu.CompilerParams(vmem_limit_bytes=48 * 2**20),
        name="finish",
    )(squares, right, right, mine, ortho, gradient, momentum)


def body(gradient, momentum, right_factor):
    ortho, mine, right, squares = make_right(right_factor, gradient, momentum)
    return finish(squares, right, mine, ortho, gradient, momentum)


def solution(mesh):
    return jax.shard_map(
        body,
        mesh=mesh,
        in_specs=(P("fsdp", "tp"), P("fsdp", "tp"), P(("tp", "fsdp"), None)),
        out_specs=(P("fsdp", "tp"), P("fsdp", "tp"), P(("tp", "fsdp"), None)),
        check_vma=False,
    )
```

```python
import functools
import math

import jax
import jax.numpy as jnp
from jax import lax
from jax.experimental import pallas as pl
from jax.experimental.pallas import tpu as pltpu
from jax.sharding import PartitionSpec as P

D = 8192
FFW = 14336
RANK = 512
N = 8
ROWS = 28
PAD = 32
HALF = 16
BLOCK = 128
MESH = pl.DeviceIdType.MESH
HIGHEST = lax.Precision.HIGHEST
VMEM = pl.BlockSpec(memory_space=pltpu.VMEM)


def params(collective_id):
    return pltpu.CompilerParams(
        collective_id=collective_id, has_side_effects=True, vmem_limit_bytes=48 * 2**20
    )


def wrap(index):
    return lax.rem(index + 2 * N, N)


def greet_start(peers):
    barrier = pltpu.get_barrier_semaphore()
    for peer in peers:
        pl.semaphore_signal(barrier, inc=1, device_id=peer, device_id_type=MESH)


def greet_end(peers):
    pl.semaphore_wait(pltpu.get_barrier_semaphore(), len(peers))


def remote(src, dst, send_sem, recv_sem, device):
    return pltpu.make_async_remote_copy(
        src_ref=src, dst_ref=dst, send_sem=send_sem, recv_sem=recv_sem,
        device_id=device, device_id_type=MESH,
    )


def place():
    fsdp = lax.axis_index("fsdp")
    return fsdp // N, lax.rem(fsdp, N), lax.axis_index("tp")


def line_device(axis, offset):
    y, z, tp = place()
    if axis == 0:
        return (wrap(y + offset) * N + z, tp)
    return (y * N + wrap(z + offset), tp)


def split(rows):
    rest = jnp.concatenate(
        [rows[HALF:], jnp.zeros((PAD - ROWS, rows.shape[1]), jnp.float32)], axis=0
    )
    return rows[:HALF].astype(jnp.bfloat16), rest.astype(jnp.bfloat16)


def tp_device(offset):
    return (lax.axis_index("fsdp"), wrap(lax.axis_index("tp") + offset))


def all_peers():
    plane = [line_device(axis, k) for axis in range(2) for k in range(1, N)]
    return plane + [tp_device(k) for k in range(1, N)]


HALVES = (pl.ds(0, N // 2), pl.ds(N // 2, N // 2))
CHAINS = [(h, d, p) for q in range(2) for h in range(2) for d in range(2) for p in [d ^ q]]


def chain_length(direction, part):
    return N // 2 if direction == part else N // 2 - 1


def signs(direction):
    return 1 - 2 * direction


def arrived(ref, sem, spare, device):
    remote(ref, ref, spare, sem, device).wait_recv()


def left_here(ref, sem, spare, device):
    remote(ref, ref, sem, spare, device).wait_send()


def exchange(source, target, send_sem, recv_sem, devices):
    for i, device in enumerate(devices):
        remote(source(i), target(i), send_sem, recv_sem, device).start()


def gather_plane(mine, out, sends, direct, landing, visit=None, beside=None):
    y, z, _ = place()
    ring, across = (y, z), (z, y)
    for k in range(1, N):
        for h in range(2):
            remote(
                mine.at[h], out.at[h, ring[h], across[h]], sends.at[0], direct.at[h],
                line_device(1 - h, k),
            ).start()
    for h in range(2):
        out[h, ring[h], across[h]] = mine[h]
    if beside is not None:
        beside(0)
    for h in range(2):
        arrived(
            out.at[h, ring[h], pl.ds(0, N - 1)], direct.at[h], sends.at[0], line_device(1 - h, 1)
        )
    arriving = {}
    device = line_device(0, 1)
    for step in range(1, N // 2 + 2):
        for h, d, p in CHAINS:
            if step == 1 and (h, d, p) == CHAINS[4]:
                if visit is not None:
                    for i, q in [(0, 0), (0, 1), (1, 0), (1, 1)]:
                        visit(i, ring[i], q)
                if beside is not None:
                    beside(1)
                left_here(out.at[:, 0], sends.at[2], direct.at[0], device)
            if 1 < step <= chain_length(d, p) + 1:
                arriving[h, d, p].wait_recv()
            if step <= chain_length(d, p):
                ref = out.at[h, wrap(ring[h] - signs(d) * (step - 1)), HALVES[p]]
                arriving[h, d, p] = remote(
                    ref, ref, sends.at[2 if step == 1 and d == p else 1],
                    landing.at[h, d, p, step - 1], line_device(h, signs(d)),
                )
                arriving[h, d, p].start()
        if visit is not None:
            for h, d, p in CHAINS:
                if 1 < step <= chain_length(d, p) + 1:
                    visit(h, wrap(ring[h] - signs(d) * (step - 1)), p)
        if beside is not None and step > 1:
            beside(step)
    left_here(out.at[:, 0, pl.ds(0, N - 1)], sends.at[0], direct.at[0], device)
    left_here(out.at[:, pl.ds(0, N - 2)], sends.at[1], direct.at[0], device)


def gather_sems():
    return [
        pltpu.SemaphoreType.DMA((3,)),
        pltpu.SemaphoreType.DMA((2,)),
        pltpu.SemaphoreType.DMA((2, 2, 2, N // 2)),
    ]


def front_part(
    factor_ref, whole_ref, left_ref, gram_ref, wide_ref,
    turned, got, partial_ref, landed, local, first, second, mine, slice_ref, padded,
    gather_sends, direct, landing, sends, recvs,
):
    y, z, tp = place()
    greet_start(all_peers())
    partial_ref[...] = jnp.zeros_like(partial_ref)
    padded[0], padded[1] = split(factor_ref[...].astype(jnp.float32))
    greet_end(all_peers())

    def arrange(step):
        if step:
            return
        turned[...] = whole_ref[...].astype(jnp.bfloat16).astype(jnp.float32).T
        for i in range(N):
            for j in range(N):
                at = (i * N + j) * ROWS
                wide_ref[0, i, j], wide_ref[1, j, i] = split(turned[at : at + ROWS, :])

    def add_terms(h, index, part):
        block = wide_ref[h, index, HALVES[part]].reshape(N // 2 * HALF, wide_ref.shape[-1])
        rows = got[h, index, HALVES[part]].reshape(N // 2 * HALF, RANK)
        partial_ref[...] += lax.dot_general(
            block, rows, (((0,), (0,)), ((), ())), preferred_element_type=jnp.float32
        )

    gather_plane(padded, got, gather_sends, direct, landing, add_terms, arrange)

    def rows(index):
        return pl.ds(pl.multiple_of(index * HALF, HALF), HALF)

    others = [tp_device(k) for k in range(1, N)]
    exchange(
        lambda i: partial_ref.at[rows(wrap(tp + i + 1))], lambda i: landed.at[i],
        sends.at[0], recvs.at[0], others,
    )
    arrived(landed, recvs.at[0], sends.at[0], others[0])
    total = partial_ref[rows(tp), :]
    for i in range(N - 1):
        total = total + landed[i]
    left_ref[rows(tp), :] = total
    exchange(
        lambda i: left_ref.at[rows(tp)], lambda i: left_ref.at[rows(tp)],
        sends.at[1], recvs.at[1], others,
    )
    most = left_ref.at[pl.ds(0, (N - 1) * HALF)]
    arrived(most, recvs.at[1], sends.at[1], others[0])

    size = RANK // N
    at = pl.ds(pl.multiple_of(tp // 2 * BLOCK, BLOCK), BLOCK)
    local[...] = full_dot(left_ref[:, at], left_ref[...], ((0,), (0,)))
    start = lax.rem(tp, 2) * size
    width = RANK // 2
    ring, across = (y, z), (z, y)

    def piece(index, base=0):
        return pl.ds(pl.multiple_of(base + index * N, N), N)

    def lanes(h):
        return pl.ds(h * width, width)

    along = [[line_device(axis, k) for k in range(1, N)] for axis in range(2)]
    for h in range(2):
        exchange(
            lambda i: local.at[piece(wrap(across[h] + i + 1), start), lanes(h)],
            lambda i: first.at[h, i], sends.at[2], recvs.at[2 + h], along[1 - h],
        )
    for h in range(2):
        arrived(first.at[h], recvs.at[2 + h], sends.at[2], others[0])
        total = local[piece(across[h], start), h * width : (h + 1) * width]
        for i in range(N - 1):
            total = total + first[h, i]
        mine[h] = total
        second[h, ring[h]] = total
        exchange(
            lambda i: mine.at[h], lambda i: second.at[h, ring[h]],
            sends.at[3], recvs.at[4 + h], along[h],
        )
    for h in range(2):
        arrived(second.at[h, pl.ds(0, N - 1)], recvs.at[4 + h], sends.at[3], others[0])
        total = second[h, 0]
        for k in range(1, N):
            total = total + second[h, k]
        slice_ref[piece(across[h]), h * width : (h + 1) * width] = total
        ref = slice_ref.at[piece(across[h]), lanes(h)]
        exchange(lambda i: ref, lambda i: ref, sends.at[4], recvs.at[6 + h], along[1 - h])
    some = pl.ds(0, (N - 1) * N)
    for h in range(2):
        arrived(slice_ref.at[some, lanes(h)], recvs.at[6 + h], sends.at[4], others[0])

    sibling = (lax.axis_index("fsdp"), tp + 1 - 2 * lax.rem(tp, 2))

    def slab(index, begin=0, count=size):
        begin = pl.multiple_of(wrap(index) * size + begin, size // 2)
        return gram_ref.at[pl.ds(begin, count)]

    far = []
    for d in range(2):
        far.append(
            remote(slice_ref, slab(tp), sends.at[5], recvs.at[8 + d], tp_device(2 * signs(d)))
        )
        far[d].start()
    remote(slice_ref, slab(tp), sends.at[5], recvs.at[12], sibling).start()
    gram_ref[pl.ds(pl.multiple_of(tp * size, size), size), :] = slice_ref[...]
    half = []
    for d in range(2):
        far[d].wait_recv()
        ref = slab(tp - 2 * signs(d), d * (size // 2), size // 2)
        half.append(remote(ref, ref, sends.at[5], recvs.at[10 + d], tp_device(2 * signs(d))))
        half[d].start()
        ref = slab(tp - 2 * signs(d))
        remote(ref, ref, sends.at[5], recvs.at[12], sibling).start()
    for d in range(2):
        half[d].wait_recv()
    ref = slab(tp + N // 2)
    remote(ref, ref, sends.at[5], recvs.at[12], sibling).start()
    arrived(gram_ref.at[pl.ds(0, N // 2 * size)], recvs.at[12], sends.at[5], sibling)

    left_here(landed, sends.at[0], recvs.at[0], sibling)
    left_here(most, sends.at[1], recvs.at[0], sibling)
    left_here(first, sends.at[2], recvs.at[0], sibling)
    left_here(second.at[:, pl.ds(0, N - 1)], sends.at[3], recvs.at[0], sibling)
    left_here(slice_ref.at[some], sends.at[4], recvs.at[0], sibling)
    left_here(gram_ref.at[pl.ds(0, (N - 1) * size)], sends.at[5], recvs.at[0], sibling)


BASE = 8


def small_inverse(panel, first):
    wide = (BASE, BLOCK)
    entry = {
        (i, j): jnp.broadcast_to(panel[i : i + 1, first + j : first + j + 1], wide)
        for i in range(BASE)
        for j in range(i + 1)
    }
    lower, inverse, scale = {}, {}, {}
    for j in range(BASE):
        pivot = entry[j, j]
        guess = lax.rsqrt(pivot)
        scale[j] = guess * (1.5 - 0.5 * ((pivot * guess) * guess))
        for i in range(j + 1, BASE):
            lower[i, j] = entry[i, j] * scale[j]
        for i in range(j + 1, BASE):
            for m in range(j + 1, i + 1):
                entry[i, m] = entry[i, m] - lower[i, j] * lower[m, j]
    for j in range(BASE):
        inverse[j, j] = scale[j]
        for i in range(j + 1, BASE):
            total = lower[i, j] * inverse[j, j]
            for m in range(j + 1, i):
                total = total + lower[i, m] * inverse[m, j]
            inverse[i, j] = -(scale[i] * total)
    index = lax.broadcasted_iota(jnp.int32, wide, 0)
    columns, rows = [], []
    for j in range(BASE):
        column = jnp.zeros(wide, jnp.float32)
        row = jnp.zeros(wide, jnp.float32)
        for i in range(j, BASE):
            column = jnp.where(index == i, inverse[i, j], column)
        for i in range(j + 1):
            row = jnp.where(index == i, inverse[j, i], row)
        columns.append(column)
        rows.append(row)
    return columns, rows


def add_up(terms):
    while len(terms) > 1:
        terms = [sum(terms[i + 1 : i + 2], terms[i]) for i in range(0, len(terms), 2)]
    return terms[0]


def combine(factors, panel):
    return [
        add_up([factors[m] * piece[m : m + 1, :] for m in range(BASE)]) for piece in panel
    ]


def block_inverse(block):
    row = lax.broadcasted_iota(jnp.int32, (BLOCK, BLOCK), 0)
    column = lax.broadcasted_iota(jnp.int32, (BLOCK, BLOCK), 1)
    unit = jnp.where(row == column, 1.0, 0.0).astype(jnp.float32)
    count = BLOCK // BASE
    panels = [
        [matrix[b * BASE : (b + 1) * BASE, :] for matrix in (block, unit)] for b in range(count)
    ]
    solved = []
    for b in range(count):
        first = b * BASE
        columns, rows = small_inverse(panels[b][0], first)
        done = combine(columns, panels[b])
        solved.append(done[1])
        if b + 1 == count:
            break
        again = combine(rows, done)
        ahead = panels[b + 1]
        factors = [
            jnp.broadcast_to(ahead[0][:, first + m : first + m + 1], (BASE, BLOCK))
            for m in range(BASE)
        ]
        panels[b + 1] = [old - new for old, new in zip(ahead, combine(factors, again))]
        if b + 2 == count:
            continue
        multiplier = jnp.concatenate([panels[c][0] for c in range(b + 2, count)], axis=0)
        parts = [jnp.concatenate(again, axis=1)]
        parts.append(jnp.zeros((BLOCK - first - BASE, 2 * BLOCK), jnp.float32))
        if first:
            parts.insert(0, jnp.zeros((first, 2 * BLOCK), jnp.float32))
        change = jnp.dot(
            multiplier, jnp.concatenate(parts, axis=0), precision=HIGHEST,
            preferred_element_type=jnp.float32,
        )
        for c in range(b + 2, count):
            at = (c - b - 2) * BASE
            panels[c] = [
                old - change[at : at + BASE, i * BLOCK : (i + 1) * BLOCK]
                for i, old in enumerate(panels[c])
            ]
    return jnp.where(row >= column, jnp.concatenate(solved, axis=0), 0.0)


def full_dot(x, y, dims):
    return lax.dot_general(
        x, y, (dims, ((), ())), precision=HIGHEST, preferred_element_type=jnp.float32
    )


def ortho_part(rest, tail, out_ref):
    for at in range(0, RANK, BLOCK):
        end = at + BLOCK
        inverse = block_inverse(rest[at:end, at:end])
        done = full_dot(tail[:, at:end], inverse, ((1,), (1,)))
        out_ref[:, at:end] = done.astype(out_ref.dtype)
        if end == RANK:
            break
        panel = full_dot(inverse, rest[at:end, end:], ((1,), (0,)))
        for start in range(end, RANK, BLOCK):
            piece = panel[:, start - end : start - end + BLOCK]
            rest[start : start + BLOCK, start:] -= full_dot(
                piece, panel[:, start - end :], ((0,), (0,))
            )
        tail[:, end:] -= full_dot(done, panel, ((1,), (0,)))


LINKS = N // 2 + 1


def right_part(
    wide_ref, ortho_ref, mine_ref, right_ref, squares_ref,
    chain, terms, summed, landed, squares, over_tp, over_line,
    gather_sends, direct, landing, sends, chain_recv, recvs,
):
    y, z, tp = place()
    ring, across = (y, z), (z, y)

    def own(h, target, part):
        block = wide_ref[h, wrap(target), HALVES[part]]
        product = jnp.dot(
            block.reshape(N // 2 * HALF, block.shape[-1]), ortho_ref[...],
            preferred_element_type=jnp.float32,
        )
        return product.reshape(N // 2, HALF, RANK)

    arriving = {}

    def slot(h, d, p, step):
        return chain.at[h, LINKS * d + step, HALVES[p]]

    def pass_on(h, d, p, step):
        arriving[h, d, p] = remote(
            slot(h, d, p, step - 1), slot(h, d, p, step),
            sends.at[3 if step == 1 and d == p else 0], chain_recv.at[h, d, p, step - 1],
            line_device(h, signs(d)),
        )
        arriving[h, d, p].start()

    def prepare(step):
        for h, d, p in CHAINS:
            if step < chain_length(d, p):
                target = ring[h] + signs(d) * (chain_length(d, p) - step)
                terms[h, d, HALVES[p]] = own(h, target, p)

    for h, d, p in CHAINS:
        term = own(h, ring[h] + signs(d) * chain_length(d, p), p)
        slot(h, d, p, 0)[...] = term.astype(jnp.bfloat16)
    device = line_device(0, 1)
    for h, d, p in CHAINS[:4]:
        pass_on(h, d, p, 1)
    prepare(1)
    left_here(chain.at[:, 0], sends.at[3], recvs.at[0], device)
    for h, d, p in CHAINS[4:]:
        pass_on(h, d, p, 1)
    for step in range(1, N // 2):
        for h, d, p in CHAINS:
            if step < chain_length(d, p):
                arriving[h, d, p].wait_recv()
                ref = slot(h, d, p, step)
                total = terms[h, d, HALVES[p]] + ref[...].astype(jnp.float32)
                ref[...] = total.astype(jnp.bfloat16)
                pass_on(h, d, p, step + 1)
        prepare(step + 1)
    for h, d, p in CHAINS[4:]:
        arriving[h, d, p].wait_recv()
        ref = slot(h, d, p, chain_length(d, p))
        terms[h, 0, HALVES[p]] = own(h, ring[h], p) + ref[...].astype(jnp.float32)
    for h in range(2):
        for i, d, p in CHAINS[:4]:
            if i == h:
                arriving[h, d, p].wait_recv()
                ref = slot(h, d, p, chain_length(d, p))
                total = terms[h, 0, HALVES[p]] + ref[...].astype(jnp.float32)
                summed[h, HALVES[p]] = total.astype(jnp.bfloat16)
        exchange(
            lambda i: summed.at[h, wrap(across[h] + i + 1)], lambda i: landed.at[h, i],
            sends.at[1], recvs.at[h], [line_device(1 - h, k) for k in range(1, N)],
        )
    for h in range(2):
        arrived(landed.at[h], recvs.at[h], sends.at[1], device)
        total = summed[h, across[h]].astype(jnp.float32)
        for i in range(N - 1):
            total = total + landed[h, i].astype(jnp.float32)
        mine_ref[h] = total.astype(jnp.bfloat16)

    def add_squares(step):
        if step == 1:
            for h in range(2):
                block = right_ref[h, ring[h]].astype(jnp.float32).reshape(N * HALF // N, N, RANK)
                total = jnp.sum(jnp.sum(block * block, axis=0), axis=0, keepdims=True)
                pieces = [total[:, c : c + BLOCK] for c in range(0, RANK, BLOCK)]
                pieces.append(jnp.zeros((N - len(pieces), BLOCK), jnp.float32))
                squares[h] = jnp.concatenate(pieces, axis=0)
            over_tp[tp] = squares[...]
            exchange(
                lambda i: squares, lambda i: over_tp.at[tp], sends.at[2], recvs.at[2],
                [tp_device(k) for k in range(1, N)],
            )
        if step == 3:
            arrived(over_tp.at[pl.ds(0, N - 1)], recvs.at[2], sends.at[2], device)
            total = over_tp[0]
            for k in range(1, N):
                total = total + over_tp[k]
            for h in range(2):
                over_line[h, ring[h]] = total[h]
                ref = over_line.at[h, ring[h]]
                exchange(
                    lambda i: ref, lambda i: ref, sends.at[4], recvs.at[3 + h],
                    [line_device(h, k) for k in range(1, N)],
                )

    gather_plane(
        mine_ref, right_ref, gather_sends, direct, landing, beside=add_squares
    )
    total = jnp.zeros((N, BLOCK), jnp.float32)
    for h in range(2):
        arrived(over_line.at[h, pl.ds(0, N - 1)], recvs.at[3 + h], sends.at[4], device)
        for k in range(N):
            total = total + over_line[h, k]
    squares_ref[...] = total
    left_here(chain.at[:, pl.ds(0, N - 2)], sends.at[0], recvs.at[0], device)
    left_here(landed, sends.at[1], recvs.at[0], device)
    left_here(over_tp.at[pl.ds(0, N - 1)], sends.at[2], recvs.at[0], device)
    left_here(over_line.at[:, pl.ds(0, N - 1)], sends.at[4], recvs.at[0], device)


FRONT_SCRATCH = [
    pltpu.VMEM((FFW // N, BLOCK), jnp.float32),
    pltpu.VMEM((2, N, N, HALF, RANK), jnp.bfloat16),
    pltpu.VMEM((BLOCK, RANK), jnp.float32),
    pltpu.VMEM((N - 1, HALF, RANK), jnp.float32),
    pltpu.VMEM((BLOCK, RANK), jnp.float32),
    pltpu.VMEM((2, N - 1, N, RANK // 2), jnp.float32),
    pltpu.VMEM((2, N, N, RANK // 2), jnp.float32),
    pltpu.VMEM((2, N, RANK // 2), jnp.float32),
    pltpu.VMEM((RANK // N, RANK), jnp.float32),
    pltpu.VMEM((2, HALF, RANK), jnp.bfloat16),
    *gather_sems(),
    pltpu.SemaphoreType.DMA((6,)),
    pltpu.SemaphoreType.DMA((13,)),
]


RIGHT_SCRATCH = [
    pltpu.VMEM((2, 2 * LINKS, N, HALF, RANK), jnp.bfloat16),
    pltpu.VMEM((2, 2, N, HALF, RANK), jnp.float32),
    pltpu.VMEM((2, N, HALF, RANK), jnp.bfloat16),
    pltpu.VMEM((2, N - 1, HALF, RANK), jnp.bfloat16),
    pltpu.VMEM((2, N, BLOCK), jnp.float32),
    pltpu.VMEM((N, 2, N, BLOCK), jnp.float32),
    pltpu.VMEM((2, N, N, BLOCK), jnp.float32),
    *gather_sems(),
    pltpu.SemaphoreType.DMA((5,)),
    pltpu.SemaphoreType.DMA((2, 2, 2, N // 2)),
    pltpu.SemaphoreType.DMA((5,)),
]


def step_kernel(
    factor_ref, whole_ref, ortho_ref, mine_ref, right_ref, squares_ref,
    left, gram, wide, *scratch,
):
    count = len(FRONT_SCRATCH)
    front_part(factor_ref, whole_ref, left, gram, wide, *scratch[:count])
    ortho_part(gram, left, ortho_ref)
    right_part(wide, ortho_ref, mine_ref, right_ref, squares_ref, *scratch[count:])


def make_right(factor, whole):
    rows = whole.shape[0]
    f32, bf16 = jnp.float32, jnp.bfloat16
    return pl.pallas_call(
        step_kernel,
        out_shape=(
            jax.ShapeDtypeStruct((rows, RANK), bf16),
            jax.ShapeDtypeStruct((2, HALF, RANK), bf16),
            jax.ShapeDtypeStruct((2, N, N, HALF, RANK), bf16),
            jax.ShapeDtypeStruct((N, BLOCK), f32),
        ),
        in_specs=[VMEM] * 2,
        out_specs=(VMEM,) * 4,
        scratch_shapes=[
            pltpu.VMEM((rows, RANK), f32),
            pltpu.VMEM((RANK, RANK), f32),
            pltpu.VMEM((2, N, N, HALF, rows), bf16),
        ]
        + FRONT_SCRATCH
        + RIGHT_SCRATCH,
        compiler_params=params(0),
        name="make_right",
    )(factor, whole)


def finish_kernel(
    squares_ref, first_ref, second_ref, mine_ref, ortho_ref, whole_ref,
    update_ref, new_ref, factor_ref, factor,
):
    squares = jnp.concatenate([squares_ref[c : c + 1, :] for c in range(RANK // BLOCK)], axis=1)
    norms = jnp.sqrt(squares + 1e-06)
    gain = math.sqrt(FFW) / norms
    ortho = ortho_ref[...]
    scaled = (ortho.astype(jnp.float32) * (norms / math.sqrt(FFW))).astype(jnp.bfloat16)
    stacked = jnp.concatenate([ortho, scaled], axis=0)
    group = 4

    def joined(top, bottom):
        top = top.astype(jnp.float32) * gain
        bottom = bottom.astype(jnp.float32) * gain
        return [top, bottom[: ROWS - HALF]]

    factor_ref[...] = jnp.concatenate(joined(mine_ref[0], mine_ref[1]), axis=0).astype(jnp.bfloat16)
    for y in range(first_ref.shape[1]):
        for z in range(0, N, group):
            pieces = []
            for i in range(z, z + group):
                pieces += joined(first_ref[0, y, i], second_ref[0, i, y])
            start = (y * N + z) * ROWS
            factor[start : start + group * ROWS, :] = jnp.concatenate(
                pieces, axis=0
            ).astype(jnp.bfloat16)
    combined = lax.dot_general(
        stacked, factor[...], (((1,), (1,)), ((), ())), preferred_element_type=jnp.float32
    )
    rows = ortho.shape[0]
    update_ref[...] = (math.sqrt(D / RANK) * combined[:rows]).astype(jnp.bfloat16)
    new_ref[...] = whole_ref[...] - 0.05 * combined[rows:]


def finish(squares, right, mine, ortho, summed):
    steps = 2
    rows, columns = summed.shape
    some = N // steps
    whole = lambda *shape: pl.BlockSpec(shape, lambda i: (0,) * len(shape))
    tile = pl.BlockSpec((rows, columns // steps), lambda i: (0, i))
    return pl.pallas_call(
        finish_kernel,
        grid=(steps,),
        out_shape=(
            jax.ShapeDtypeStruct((rows, columns), jnp.bfloat16),
            jax.ShapeDtypeStruct((rows, columns), jnp.float32),
            jax.ShapeDtypeStruct((ROWS, RANK), jnp.bfloat16),
        ),
        in_specs=[
            whole(N, BLOCK),
            pl.BlockSpec((1, some, N, HALF, RANK), lambda i: (0, i, 0, 0, 0)),
            pl.BlockSpec((1, N, some, HALF, RANK), lambda i: (1, 0, i, 0, 0)),
            whole(2, HALF, RANK),
            whole(rows, RANK),
            tile,
        ],
        out_specs=(tile, tile, whole(ROWS, RANK)),
        scratch_shapes=[pltpu.VMEM((columns // steps, RANK), jnp.bfloat16)],
        compiler_params=pltpu.CompilerParams(vmem_limit_bytes=48 * 2**20),
        name="finish",
    )(squares, right, right, mine, ortho, summed)


def body(gradient, momentum, right_factor):
    whole = momentum + gradient.astype(jnp.float32)
    ortho, mine, right, squares = make_right(right_factor, whole)
    return finish(squares, right, mine, ortho, whole)


def solution(mesh):
    return jax.shard_map(
        body,
        mesh=mesh,
        in_specs=(P("fsdp", "tp"), P("fsdp", "tp"), P(("tp", "fsdp"), None)),
        out_specs=(P("fsdp", "tp"), P("fsdp", "tp"), P(("tp", "fsdp"), None)),
        check_vma=False,
    )
```
